32 devices in a mesh: region: 8 (over z, x), mp: 4 (over y, core).
Axes of the slice: x: 2, y: 2, z: 4, core: 2. Of those that a mesh axis runs over, the one named last changes fastest.
Arguments:
- tile_data: bfloat16 [32, 256, 2048], P('region', None, 'mp'), may hold values from -6.5 to 6.5
- tile_counts: int32 [8], replicated, may hold values from 0 to 4, as said below
- modulation: bfloat16 [8, 3, 2048], P('region'), may hold values from -4 to 4
- qkv_weight: bfloat16 [2048, 3, 2048], P('region', None, 'mp'), may hold values from -0.92807765 to 0.92807765
- out_weight: bfloat16 [2048, 2048], P('region', 'mp'), may hold values from -0.125 to 0.125
- blend_weights: float32 [6], replicated, may hold values from 0.1 to 0.9
Outputs:
- blended: bfloat16 [32, 256, 2048], P('region', None, 'mp')
The draws below stay inside these ranges and needn't reach their ends.
Inputs may be any that keep to these rules, and one draw needn't show every extreme that they name: `tile_counts`: groups 2m and 2m + 1 together hold exactly 4 tiles. In every draw some group holds 4 tiles and its partner none.
All inputs are finite; a program needn't handle non-finite values.
Results may differ from the reference program's by a relative error of at most 0.0071.
Values may be sent and summed in bfloat16 or wider, within the bound.
A program may use at most 64 MiB of HBM per device.

```python
import math
import jax
import jax.numpy as jnp
from jax import lax

D = 2048
HEADS = 16
HDIM = 128
S = 16
TOK = 256
W = 6
TCOLS = 8
TPD = 2
PAIRT = 4
GROUPS = 8


def draw_tile_data(key, part):
    key = jax.random.fold_in(key, 11)
    normal_part = jnp.clip(jax.random.normal(key, (GROUPS * PAIRT, TOK, D), jnp.float32), -6.0, 6.0)
    return normal_part.astype(jnp.bfloat16)


def draw_tile_counts(key, part):
    key = jax.random.fold_in(key, 37)
    pair_total = GROUPS // 2
    even_counts = jax.random.randint(key, (pair_total,), 0, PAIRT + 1)
    chosen = jax.random.randint(jax.random.fold_in(key, 1), (), 0, pair_total)
    extreme = jax.random.randint(jax.random.fold_in(key, 2), (), 0, 2) * PAIRT
    even_counts = jnp.where(jnp.arange(pair_total) == chosen, extreme, even_counts)
    return jnp.stack([even_counts, PAIRT - even_counts], axis=1).reshape(GROUPS).astype(jnp.int32)


def draw_qkv_weight(key, part):
    key = jax.random.fold_in(key, 23)
    normal_part = jnp.clip(jax.random.normal(key, (D, 3, D), jnp.float32), -4.0, 4.0)
    return (normal_part / math.sqrt(D)).astype(jnp.bfloat16)


def level_of(own_key, dims, shards, smallest, largest):
    gain = 1.0
    for axis_at, blocks in shards:
        draws = jax.random.uniform(jax.random.fold_in(jax.random.fold_in(own_key, 6), axis_at), (blocks,), jnp.float32, smallest / len(shards), largest / len(shards))
        gain = gain * jnp.repeat(jnp.exp(draws), dims[axis_at] // blocks).reshape((-1,) + (1,) * (len(dims) - 1 - axis_at))
    return gain


def scatter_about(rng, dims, width, limit, shards=(), kind=jnp.bfloat16):
    array = width * jax.random.normal(rng, dims, jnp.float32)
    if shards:
        array = array * level_of(rng, dims, shards, -0.22, 0.18)
    return jnp.clip(array, -limit, limit).astype(kind)


def setup_inputs(seed: int = 0) -> dict:
    key_list = jax.random.split(jax.random.key(seed), 7)
    return {
        "tile_data": draw_tile_data(jax.random.fold_in(key_list[6], 71), 0),
        "tile_counts": draw_tile_counts(jax.random.fold_in(key_list[6], 71), 0),
        "modulation": scatter_about(key_list[2], (GROUPS, 3, D), 1.0, 4.0, ((0, 8),)),
        "qkv_weight": draw_qkv_weight(jax.random.fold_in(key_list[6], 71), 0),
        "out_weight": scatter_about(key_list[4], (D, D), D ** -0.5, 0.125, ((0, 8), (1, 4))),
        "blend_weights": jnp.clip(jax.random.uniform(key_list[5], (W,), jnp.float32, 0.1, 0.9), 0.1, 0.9),
    }


def normalise(values):
    row_mean = lax.optimization_barrier(jnp.mean(values, axis=-1, keepdims=True))
    centred = values - row_mean
    spread = lax.optimization_barrier(jnp.mean(centred * centred, axis=-1, keepdims=True))
    return centred * lax.rsqrt(spread + 1e-06)

def one_tile(tile_rows, modulators, qkv_weight, out_weight):
    values = tile_rows.astype(jnp.float32)
    mod_values = modulators.astype(jnp.float32)
    hidden = (normalise(values) * (1.0 + mod_values[1]) + mod_values[0]).astype(jnp.bfloat16)
    projections = jnp.dot(hidden, qkv_weight.reshape(D, 3 * D), preferred_element_type=jnp.float32)
    projections = lax.optimization_barrier(projections.astype(jnp.bfloat16))
    projections = projections.astype(jnp.float32).reshape(TOK, 3, HEADS, HDIM)
    scores = jnp.einsum('qhe,khe->hqk', projections[:, 0], projections[:, 1]) / math.sqrt(HDIM)
    attention_weights = lax.optimization_barrier(jax.nn.softmax(scores, axis=-1).astype(jnp.bfloat16))
    attended = jnp.einsum('hqk,khe->qhe', attention_weights.astype(jnp.float32), projections[:, 2])
    attended = attended.astype(jnp.bfloat16).reshape(TOK, D)
    projected = jnp.dot(attended, out_weight.T, preferred_element_type=jnp.float32)
    return (values + mod_values[2] * projected).astype(jnp.bfloat16)

def reference(tile_data, tile_counts, modulation, qkv_weight, out_weight, blend_weights):
    tile_total = TPD * tile_counts.shape[0]
    group_ends = jnp.cumsum(tile_counts).astype(jnp.int32)
    group_starts = (group_ends - tile_counts).astype(jnp.int32)
    tile_ids = jnp.arange(tile_total, dtype=jnp.int32)
    owner_ids = lax.optimization_barrier(jnp.sum((group_ends[None, :] <= tile_ids[:, None]).astype(jnp.int32), axis=1)).astype(jnp.int32)
    slot_ids = (tile_ids - group_starts[owner_ids]).astype(jnp.int32)
    slot_rows = (owner_ids * PAIRT + slot_ids).astype(jnp.int32)

    def process(carried):
        return one_tile(tile_data[carried[0]], modulation[carried[1]], qkv_weight, out_weight)
    updated = lax.map(process, (slot_rows, owner_ids))
    tile_grid = updated.reshape(tile_total // TCOLS, TCOLS, S, S, D).astype(jnp.float32)
    shares = blend_weights.astype(jnp.float32)
    across = shares[None, None, None, :, None]
    mixture = (1.0 - across) * tile_grid[:, :-1, :, S - W:, :] + across * tile_grid[:, 1:, :, :W, :]
    joined = tile_grid.at[:, :-1, :, S - W:, :].set(mixture).at[:, 1:, :, :W, :].set(mixture)
    joined = lax.optimization_barrier(joined.astype(jnp.bfloat16)).astype(jnp.float32)
    downward = shares[None, None, :, None, None]
    mixture = (1.0 - downward) * joined[:-1, :, S - W:, :, :] + downward * joined[1:, :, :W, :, :]
    finished = joined.at[:-1, :, S - W:, :, :].set(mixture).at[1:, :, :W, :, :].set(mixture)
    finished = finished.astype(jnp.bfloat16).reshape(tile_total, TOK, D)
    output = jnp.zeros(tile_data.shape, jnp.bfloat16).at[slot_rows].set(finished)
    return output
```

```python
import functools
import math

import jax
import jax.numpy as jnp
from jax import lax
from jax.experimental import pallas as pl
from jax.experimental.pallas import tpu as pltpu
from jax.sharding import PartitionSpec as P

HDIM = 128
S = 16
W = 6
TCOLS = 8
MESH = pl.DeviceIdType.MESH
F32 = jnp.float32
BF16 = jnp.bfloat16


def kernel(
    regions,
    counts_ref,
    blend_ref,
    tiles_ref,
    mod_ref,
    wqkv_ref,
    wout_ref,
    out_ref,
    slots,
    feats,
    mods,
    wq,
    wo,
    hidden,
    attended,
    part_near,
    part_far,
    from_core,
    from_far,
    updated,
    side,
    strips,
    finished,
    partner_done,
    swap_send,
    swap_recv,
    gather_send,
    gather_recv,
    line_send,
    line_recv,
    sum_send,
    sum_recv,
    edge_send,
    edge_recv,
):
    planes = regions // 2
    region = lax.axis_index("region")
    mp = lax.axis_index("mp")
    plane = region // 2
    x = region % 2
    xo = 1 - x
    partner = plane * 2 + xo
    core = mp % 2
    yy = mp // 2
    mp_core = yy * 2 + (1 - core)
    mp_y = (1 - yy) * 2 + core
    nslot, tok, wide = tiles_ref.shape
    fb = wide // 2
    rows = wqkv_ref.shape[1]
    down = TCOLS // nslot
    mine = mp * 2 + x
    has_up = plane > 0
    has_down = plane < planes - 1
    far_up = plane >= down
    far_down = plane < planes - down

    barrier = pltpu.get_barrier_semaphore()

    def greet(r, m):
        pl.semaphore_signal(barrier, inc=1, device_id=(r, m), device_id_type=MESH)

    greet(region, mp_core)
    greet(region, mp_y)
    greet(partner, mp)
    greet(partner, mp_y)
    for cond, step in ((has_up, -2), (has_down, 2), (far_up, -2 * down), (far_down, 2 * down)):

        @pl.when(cond)
        def _(step=step):
            greet(region + step, mp)

    arrivals = (
        4
        + has_up.astype(jnp.int32)
        + has_down.astype(jnp.int32)
        + far_up.astype(jnp.int32)
        + far_down.astype(jnp.int32)
    )
    pl.semaphore_wait(barrier, arrivals)

    def remote(src, dst, ssem, rsem, r, m):
        return pltpu.make_async_remote_copy(
            src_ref=src, dst_ref=dst, send_sem=ssem, recv_sem=rsem, device_id=(r, m), device_id_type=MESH
        )

    def block(buf, r):
        return buf.at[pl.ds(pl.multiple_of(r * rows, rows), rows)]

    def swap(i, src, dst):
        return remote(src, dst, swap_send.at[i], swap_recv.at[i], partner, mp)

    half_o = pl.ds(pl.multiple_of(xo * fb, fb), fb)
    half_m = pl.ds(pl.multiple_of(x * fb, fb), fb)

    def swaps(r, g):
        return (
            swap(0, wqkv_ref.at[xo], block(wq, r)),
            swap(1, tiles_ref.at[:, :, half_o], slots.at[g]),
            swap(2, mod_ref, mods.at[g]),
            swap(3, wout_ref.at[xo], block(wo, r)),
        )

    out_swaps = swaps(region, x)
    in_swaps = swaps(partner, xo)
    for c in out_swaps:
        c.start()
    block(wq, region)[...] = wqkv_ref[x]
    block(wo, region)[...] = wout_ref[x]
    mods[x] = mod_ref[...]
    slots[x] = tiles_ref[:, :, half_m]

    def line(buf, kind, way, s, h, q):
        ref = block(buf, 2 * q + h)
        step = 2 if way == 0 else -2
        return remote(
            ref, ref, line_send.at[way, kind, s, h], line_recv.at[way, kind, s, h], region + step, mp
        )

    def line_do(buf, kind, s, h, act):
        @pl.when(has_down & (plane - s >= 0))
        def _():
            act(line(buf, kind, 0, s, h, plane - s))

        @pl.when(has_up & (plane + s <= planes - 1))
        def _():
            act(line(buf, kind, 1, s, h, plane + s))

    def line_send_start(buf, kind, s, h):
        line_do(buf, kind, s, h, lambda c: c.start())

    def line_wait_recv(buf, kind, s):
        @pl.when(plane - s - 1 >= 0)
        def _():
            for h in range(2):
                line(buf, kind, 0, s, h, plane - s - 1).wait_recv()

        @pl.when(plane + s + 1 <= planes - 1)
        def _():
            for h in range(2):
                line(buf, kind, 1, s, h, plane + s + 1).wait_recv()

    def line_forward(buf, kind, s):
        line_wait_recv(buf, kind, s)

        @pl.when(s + 1 < planes - 1)
        def _():
            for h in range(2):
                line_send_start(buf, kind, s + 1, h)

    line_send_start(wq, 0, 0, x)
    in_swaps[0].wait_recv()
    line_send_start(wq, 0, 0, xo)

    in_swaps[1].wait_recv()
    even = counts_ref[2 * plane]
    own_count = counts_ref[region]
    for k in range(nslot):
        first = slots[0, k]
        second = slots[1, jnp.clip(k - even, 0, nslot - 1)]
        feats[mine, k] = jnp.where(k < even, first, second)

    def gather(i, b, r, m):
        return remote(feats.at[b], feats.at[b], gather_send.at[i], gather_recv.at[i], r, m)

    blocks = (mp * 2 + xo, mp_y * 2 + x, mp_y * 2 + xo)
    core_blocks = (mp_core * 2 + x, mp_core * 2 + xo, (3 - mp) * 2 + x, (3 - mp) * 2 + xo)
    sends = [
        gather(0, mine, partner, mp),
        gather(1, mine, region, mp_y),
        gather(2, mine, partner, mp_y),
        gather(3, mine, region, mp_core),
    ]
    for c in (sends[2], sends[0], sends[1], sends[3]):
        c.start()
    line_forward(wq, 0, 0)
    for i in range(3):
        gather(i, blocks[i], region, mp_core).wait_recv()
        c = gather(4 + i, blocks[i], region, mp_core)
        c.start()
        sends.append(c)
    in_swaps[2].wait_recv()
    in_swaps[3].wait_recv()
    for i in range(4):
        gather(3 + i, core_blocks[i], region, mp_core).wait_recv()

    nblock = feats.shape[0]
    inv = 1.0 / (nblock * fb)
    mod_e = mods[0].astype(F32)
    mod_d = mods[1].astype(F32)

    def normalise(t, _):
        total = jnp.zeros((tok, 1), F32)
        for b in range(nblock):
            total = total + jnp.sum(feats[b, t].astype(F32), axis=1, keepdims=True)
        mean = total * inv
        total = jnp.zeros((tok, 1), F32)
        for b in range(nblock):
            c = feats[b, t].astype(F32) - mean
            total = total + jnp.sum(c * c, axis=1, keepdims=True)
        scale = lax.rsqrt(total * inv + 1e-06)
        mod = jnp.where(t < even, mod_e, mod_d)
        for b in range(nblock):
            at = slice(b * fb, (b + 1) * fb)
            c = (feats[b, t].astype(F32) - mean) * scale
            hidden[t, :, at] = (c * (1.0 + mod[1:2, at]) + mod[0:1, at]).astype(BF16)
        return 0

    @pl.when(planes > 2)
    def _():
        line_forward(wq, 0, 1)

    lax.fori_loop(0, nslot, normalise, 0)

    def more(s, _):
        line_forward(wq, 0, s)
        return 0

    lax.fori_loop(2, planes - 1, more, 0)
    for h in range(2):
        line_send_start(wo, 1, 0, h)

    heads = fb // HDIM

    def attend(t, _):
        proj = jnp.dot(hidden[t], wq[...], preferred_element_type=F32).astype(BF16)
        for h in range(heads):
            q = proj[:, h * HDIM : (h + 1) * HDIM]
            k = proj[:, fb + h * HDIM : fb + (h + 1) * HDIM]
            v = proj[:, 2 * fb + h * HDIM : 2 * fb + (h + 1) * HDIM]
            scores = lax.dot_general(q, k, (((1,), (1,)), ((), ())), preferred_element_type=F32)
            scores = scores * (1.0 / math.sqrt(HDIM))
            e = jnp.exp(scores - jnp.max(scores, axis=-1, keepdims=True))
            p = (e / jnp.sum(e, axis=-1, keepdims=True)).astype(BF16)
            attended[t, :, h * HDIM : (h + 1) * HDIM] = jnp.dot(
                p, v, preferred_element_type=F32
            ).astype(BF16)

        @pl.when(t < planes - 1)
        def _():
            line_forward(wo, 1, t)

        return 0

    lax.fori_loop(0, nslot, attend, 0)

    def rest(s, _):
        line_forward(wo, 1, s)
        return 0

    if planes - 1 > nslot:
        lax.fori_loop(nslot, planes - 1, rest, 0)

    def product(b, t):
        w = wo[pl.ds(pl.multiple_of(b * fb, fb), fb)]
        return lax.dot_general(attended[t], w, (((1,), (1,)), ((), ())), preferred_element_type=F32)

    dests = ((xo, mp_y), (x, mp_y), (xo, mp), (x, mp))

    def core_sum(i):
        return remote(
            part_near.at[i], from_core.at[i], sum_send.at[i], sum_recv.at[i], region, mp_core
        )

    def far_sum(i):
        dx, dm = dests[i]
        return remote(
            part_far.at[i], from_far.at[i], sum_send.at[4 + i], sum_recv.at[4 + i], plane * 2 + dx, dm
        )

    for i, (dx, dm) in enumerate(dests):
        b = (dm + 1 - 2 * core) * 2 + dx

        def near(t, _, i=i, b=b):
            part_near[i, t] = product(b, t).astype(BF16)
            return 0

        lax.fori_loop(0, nslot, near, 0)
        core_sum(i).start()
    for i, (dx, dm) in enumerate(dests[:3]):
        b = dm * 2 + dx
        core_sum(i).wait_recv()

        def far(t, _, i=i, b=b):
            part_far[i, t] = (product(b, t) + from_core[i, t].astype(F32)).astype(BF16)
            return 0

        lax.fori_loop(0, nslot, far, 0)
        far_sum(i).start()
    core_sum(3).wait_recv()
    for i in range(3):
        far_sum(i).wait_recv()
    at_m = pl.ds(pl.multiple_of(mine * fb, fb), fb)
    gate_e = mods[0, :, at_m].astype(F32)[2:3]
    gate_d = mods[1, :, at_m].astype(F32)[2:3]

    def update(t, _):
        total = product(mine, t) + from_core[3, t].astype(F32)
        for i in range(3):
            total = total + from_far[i, t].astype(F32)
        gate = jnp.where(t < even, gate_e, gate_d)
        updated[t] = (feats[mine, t].astype(F32) + gate * total).astype(BF16)
        return 0

    lax.fori_loop(0, nslot, update, 0)

    odd = plane % 2
    edge_tile = (1 - odd) * (nslot - 1)
    to_side = remote(
        updated.at[edge_tile],
        side,
        edge_send.at[0],
        edge_recv.at[0],
        region + 2 - 4 * odd,
        mp,
    )
    to_side.start()
    token = lax.broadcasted_iota(jnp.int32, (tok, fb), 0)
    col = token % S
    share = jnp.zeros((tok, fb), F32)
    for k in range(W):
        share = jnp.where((col == k) | (col == S - W + k), blend_ref[k], share)
    near_cols = col < W
    far_cols = col >= S - W
    to_side.wait_recv()
    plain = [updated[k].astype(F32) for k in range(nslot)]
    edge = side[...].astype(F32)
    for k in range(nslot):
        own = plain[k]
        if k > 0:
            left, has_left = plain[k - 1], True
        else:
            left, has_left = edge, odd == 1
        if k < nslot - 1:
            right, has_right = plain[k + 1], True
        else:
            right, has_right = edge, odd == 0
        left = pltpu.roll(left, tok - (S - W), 0)
        right = pltpu.roll(right, S - W, 0)
        new = jnp.where(near_cols & has_left, (1.0 - share) * left + share * own, own)
        new = jnp.where(far_cols & has_right, (1.0 - share) * own + share * right, new)
        finished[k] = new.astype(BF16)

    reach = W * S
    low = pl.ds(0, reach)
    high = pl.ds(tok - reach, reach)

    def to_above():
        return remote(
            finished.at[:, low],
            strips.at[0],
            edge_send.at[1],
            edge_recv.at[1],
            region - 2 * down,
            mp,
        )

    def to_below():
        return remote(
            finished.at[:, high],
            strips.at[1],
            edge_send.at[2],
            edge_recv.at[2],
            region + 2 * down,
            mp,
        )

    @pl.when(far_up)
    def _():
        to_above().start()

    @pl.when(far_down)
    def _():
        to_below().start()

    row = lax.broadcasted_iota(jnp.int32, (reach, fb), 0) // S
    vshare = jnp.zeros((reach, fb), F32)
    for k in range(W):
        vshare = jnp.where(row == k, blend_ref[k], vshare)

    @pl.when(far_up)
    def _():
        to_above().wait_send()
        to_below().wait_recv()
        for k in range(nslot):
            own = finished[k, low].astype(F32)
            finished[k, low] = ((1.0 - vshare) * strips[1, k].astype(F32) + vshare * own).astype(BF16)

    @pl.when(far_down)
    def _():
        to_below().wait_send()
        to_above().wait_recv()
        for k in range(nslot):
            own = finished[k, high].astype(F32)
            finished[k, high] = ((1.0 - vshare) * own + vshare * strips[0, k].astype(F32)).astype(BF16)

    last = remote(finished, partner_done, edge_send.at[3], edge_recv.at[3], partner, mp)
    last.start()
    start = x * even
    for s in range(nslot):
        got = finished[jnp.clip(start + s, 0, nslot - 1)]
        out_ref[s, :, half_m] = jnp.where(s < own_count, got, jnp.zeros_like(got))
    last.wait_recv()
    for s in range(nslot):
        got = partner_done[jnp.clip(start + s, 0, nslot - 1)]
        out_ref[s, :, half_o] = jnp.where(s < own_count, got, jnp.zeros_like(got))

    last.wait_send()
    to_side.wait_send()
    for c in out_swaps:
        c.wait_send()
    for c in sends:
        c.wait_send()
    for i in range(4):
        core_sum(i).wait_send()
    for i in range(3):
        far_sum(i).wait_send()

    def drain(s, _):
        for kind, buf in ((0, wq), (1, wo)):
            for h in range(2):
                line_do(buf, kind, s, h, lambda c: c.wait_send())
        return 0

    lax.fori_loop(0, planes - 1, drain, 0)


def on_device(regions, tile_data, tile_counts, modulation, qkv_weight, out_weight, blend_weights):
    nslot, tok, wide = tile_data.shape
    rows, kinds, _ = qkv_weight.shape
    fb = wide // 2
    width = modulation.shape[2]
    nblock = width // fb
    planes = regions // 2
    wqkv = qkv_weight.reshape(rows, kinds, 2, fb).transpose(2, 0, 1, 3).reshape(2, rows, kinds * fb)
    wout = out_weight.reshape(rows, 2, fb).transpose(1, 0, 2)
    mod = jnp.pad(modulation[0], ((0, 13), (0, 0)))
    vmem = pl.BlockSpec(memory_space=pltpu.VMEM)
    smem = pl.BlockSpec(memory_space=pltpu.SMEM)
    dma = pltpu.SemaphoreType.DMA
    return pl.pallas_call(
        functools.partial(kernel, regions),
        out_shape=jax.ShapeDtypeStruct(tile_data.shape, BF16),
        in_specs=[smem, smem, vmem, vmem, vmem, vmem],
        out_specs=vmem,
        scratch_shapes=[
            pltpu.VMEM((2, nslot, tok, fb), BF16),
            pltpu.VMEM((nblock, nslot, tok, fb), BF16),
            pltpu.VMEM((2, 16, width), BF16),
            pltpu.VMEM((width, kinds * fb), BF16),
            pltpu.VMEM((width, fb), BF16),
            pltpu.VMEM((nslot, tok, width), BF16),
            pltpu.VMEM((nslot, tok, fb), BF16),
            pltpu.VMEM((4, nslot, tok, fb), BF16),
            pltpu.VMEM((3, nslot, tok, fb), BF16),
            pltpu.VMEM((4, nslot, tok, fb), BF16),
            pltpu.VMEM((3, nslot, tok, fb), BF16),
            pltpu.VMEM((nslot, tok, fb), BF16),
            pltpu.VMEM((tok, fb), BF16),
            pltpu.VMEM((2, nslot, W * S, fb), BF16),
            pltpu.VMEM((nslot, tok, fb), BF16),
            pltpu.VMEM((nslot, tok, fb), BF16),
            dma((4,)),
            dma((4,)),
            dma((7,)),
            dma((7,)),
            dma((2, 2, planes - 1, 2)),
            dma((2, 2, planes - 1, 2)),
            dma((7,)),
            dma((7,)),
            dma((4,)),
            dma((4,)),
        ],
        compiler_params=pltpu.CompilerParams(
            collective_id=0, has_side_effects=True, vmem_limit_bytes=56 * 1024 * 1024
        ),
    )(tile_counts, blend_weights, tile_data, mod, wqkv, wout)


def solution(mesh):
    return jax.shard_map(
        functools.partial(on_device, mesh.shape["region"]),
        mesh=mesh,
        in_specs=(
            P("region", None, "mp"),
            P(),
            P("region", None, None),
            P("region", None, "mp"),
            P("region", "mp"),
            P(),
        ),
        out_specs=P("region", None, "mp"),
        check_vma=False,
    )
```

```python
import functools
import math

import jax
import jax.numpy as jnp
from jax import lax
from jax.experimental import pallas as pl
from jax.experimental.pallas import tpu as pltpu
from jax.sharding import PartitionSpec as P

HDIM = 128
S = 16
W = 6
TCOLS = 8
MESH = pl.DeviceIdType.MESH
F32 = jnp.float32
BF16 = jnp.bfloat16


def kernel(
    regions,
    counts_ref,
    blend_ref,
    tiles_ref,
    mod_ref,
    wqkv_ref,
    wout_ref,
    out_ref,
    slots,
    feats,
    mods,
    stage,
    wq,
    wo,
    hidden,
    attended,
    part_near,
    part_far,
    from_core,
    from_far,
    updated,
    side,
    strips,
    finished,
    partner_done,
    swap_send,
    swap_recv,
    gather_send,
    gather_recv,
    line_send,
    line_recv,
    near_send,
    near_recv,
    sum_send,
    sum_recv,
    edge_send,
    edge_recv,
    strip_send,
    strip_recv,
    last_send,
    last_recv,
):
    planes = regions // 2
    region = lax.axis_index("region")
    mp = lax.axis_index("mp")
    plane = region // 2
    x = region % 2
    xo = 1 - x
    partner = plane * 2 + xo
    core = mp % 2
    yy = mp // 2
    mp_core = yy * 2 + (1 - core)
    mp_y = (1 - yy) * 2 + core
    nslot, tok, wide = tiles_ref.shape
    fb = wide // 2
    rows = wqkv_ref.shape[0]
    kinds = wqkv_ref.shape[1] // wide
    down = TCOLS // nslot
    mine = mp * 2 + x
    has_up = plane > 0
    has_down = plane < planes - 1
    far_up = plane >= down
    far_down = plane < planes - down

    barrier = pltpu.get_barrier_semaphore()

    def greet(r, m):
        pl.semaphore_signal(barrier, inc=1, device_id=(r, m), device_id_type=MESH)

    greet(region, mp_core)
    greet(region, mp_y)
    greet(partner, mp)
    greet(partner, mp_y)
    for cond, step in ((has_up, -2), (has_down, 2), (far_up, -2 * down), (far_down, 2 * down)):

        @pl.when(cond)
        def _(step=step):
            greet(region + step, mp)

    arrivals = (
        4
        + has_up.astype(jnp.int32)
        + has_down.astype(jnp.int32)
        + far_up.astype(jnp.int32)
        + far_down.astype(jnp.int32)
    )
    pl.semaphore_wait(barrier, arrivals)

    def remote(src, dst, ssem, rsem, r, m):
        return pltpu.make_async_remote_copy(
            src_ref=src, dst_ref=dst, send_sem=ssem, recv_sem=rsem, device_id=(r, m), device_id_type=MESH
        )

    def block(buf, r):
        return buf.at[pl.ds(pl.multiple_of(r * rows, rows), rows)]

    def swap(i, src, dst):
        return remote(src, dst, swap_send.at[i], swap_recv.at[i], partner, mp)

    half_o = pl.ds(pl.multiple_of(xo * fb, fb), fb)
    half_m = pl.ds(pl.multiple_of(x * fb, fb), fb)

    def swaps(r, g):
        return (
            swap(0, stage, block(wq, r)),
            swap(1, tiles_ref.at[:, :, half_o], slots.at[g]),
            swap(2, mods.at[g], mods.at[g]),
            swap(3, wout_ref.at[:, half_o], block(wo, r)),
        )

    out_swaps = swaps(region, x)
    in_swaps = swaps(partner, xo)
    for k in range(kinds):
        at = pl.ds(pl.multiple_of(k * wide + xo * fb, fb), fb)
        stage[:, k * fb : (k + 1) * fb] = wqkv_ref[:, at]
    out_swaps[0].start()
    for k in range(kinds):
        at = pl.ds(pl.multiple_of(k * wide + x * fb, fb), fb)
        wq[pl.ds(pl.multiple_of(region * rows, rows), rows), k * fb : (k + 1) * fb] = wqkv_ref[:, at]

    def line(buf, kind, way, s, h, q):
        ref = block(buf, 2 * q + h)
        step = 2 if way == 0 else -2
        return remote(
            ref, ref, line_send.at[way, kind, s, h], line_recv.at[way, kind, s, h], region + step, mp
        )

    def line_do(buf, kind, s, h, act):
        @pl.when(has_down & (plane - s >= 0))
        def _():
            act(line(buf, kind, 0, s, h, plane - s))

        @pl.when(has_up & (plane + s <= planes - 1))
        def _():
            act(line(buf, kind, 1, s, h, plane + s))

    def line_send_start(buf, kind, s, h):
        line_do(buf, kind, s, h, lambda c: c.start())

    def line_wait_recv(buf, kind, s):
        @pl.when(plane - s - 1 >= 0)
        def _():
            for h in range(2):
                line(buf, kind, 0, s, h, plane - s - 1).wait_recv()

        @pl.when(plane + s + 1 <= planes - 1)
        def _():
            for h in range(2):
                line(buf, kind, 1, s, h, plane + s + 1).wait_recv()

    def line_forward(buf, kind, s):
        line_wait_recv(buf, kind, s)

        @pl.when(s + 1 < planes - 1)
        def _():
            for h in range(2):
                line_send_start(buf, kind, s + 1, h)

    line_send_start(wq, 0, 0, x)
    block(wo, region)[...] = wout_ref[:, half_m]
    mods[x, 0:3, :] = mod_ref[0]
    slots[x] = tiles_ref[:, :, half_m]
    in_swaps[0].wait_recv()
    line_send_start(wq, 0, 0, xo)
    for c in out_swaps[1:]:
        c.start()

    in_swaps[1].wait_recv()
    even = counts_ref[2 * plane]
    own_count = counts_ref[region]
    for k in range(nslot):
        first = slots[0, k]
        second = slots[1, jnp.clip(k - even, 0, nslot - 1)]
        feats[mine, k] = jnp.where(k < even, first, second)

    def gather(i, b, r, m):
        return remote(feats.at[b], feats.at[b], gather_send.at[i], gather_recv.at[i], r, m)

    blocks = (mp * 2 + xo, mp_y * 2 + x, mp_y * 2 + xo)
    core_blocks = (mp_core * 2 + x, mp_core * 2 + xo, (3 - mp) * 2 + x, (3 - mp) * 2 + xo)
    sends = [
        gather(0, mine, partner, mp),
        gather(1, mine, region, mp_y),
        gather(2, mine, partner, mp_y),
        gather(3, mine, region, mp_core),
    ]
    for c in (sends[2], sends[0], sends[1], sends[3]):
        c.start()
    line_forward(wq, 0, 0)
    in_swaps[2].wait_recv()
    in_swaps[3].wait_recv()
    for h in range(2):
        line_send_start(wo, 1, 0, h)

    line_forward(wq, 0, 1)
    if planes > 3:
        line_forward(wo, 1, 0)
    for i in range(3):
        gather(i, blocks[i], region, mp_core).wait_recv()
        c = gather(4 + i, blocks[i], region, mp_core)
        c.start()
        sends.append(c)
    for i in range(4):
        gather(3 + i, core_blocks[i], region, mp_core).wait_recv()

    nblock = feats.shape[0]
    inv = 1.0 / (nblock * fb)
    mod_e = mods[0].astype(F32)
    mod_d = mods[1].astype(F32)

    def normalise(t, _):
        total = jnp.zeros((tok, 1), F32)
        for b in range(nblock):
            total = total + jnp.sum(feats[b, t].astype(F32), axis=1, keepdims=True)
        mean = total * inv
        total = jnp.zeros((tok, 1), F32)
        for b in range(nblock):
            c = feats[b, t].astype(F32) - mean
            total = total + jnp.sum(c * c, axis=1, keepdims=True)
        scale = lax.rsqrt(total * inv + 1e-06)
        mod = jnp.where(t < even, mod_e, mod_d)
        for b in range(nblock):
            at = slice(b * fb, (b + 1) * fb)
            c = (feats[b, t].astype(F32) - mean) * scale
            hidden[t, :, at] = (c * (1.0 + mod[1:2, at]) + mod[0:1, at]).astype(BF16)
        return 0

    lax.fori_loop(0, nslot, normalise, 0)

    def more(s, _):
        line_forward(wo, 1, s - 1)
        line_forward(wq, 0, s)
        return 0

    lax.fori_loop(2, planes - 2, more, 0)
    line_forward(wq, 0, planes - 2)

    heads = fb // HDIM

    def attend(t, _):
        proj = jnp.dot(hidden[t], wq[...], preferred_element_type=F32).astype(BF16)
        for h in range(heads):
            q = proj[:, h * HDIM : (h + 1) * HDIM]
            k = proj[:, fb + h * HDIM : fb + (h + 1) * HDIM]
            v = proj[:, 2 * fb + h * HDIM : 2 * fb + (h + 1) * HDIM]
            scores = lax.dot_general(q, k, (((1,), (1,)), ((), ())), preferred_element_type=F32)
            scores = scores * (1.0 / math.sqrt(HDIM))
            e = jnp.exp(scores - jnp.max(scores, axis=-1, keepdims=True))
            p = (e / jnp.sum(e, axis=-1, keepdims=True)).astype(BF16)
            attended[t, :, h * HDIM : (h + 1) * HDIM] = jnp.dot(
                p, v, preferred_element_type=F32
            ).astype(BF16)

        return 0

    odd = plane % 2

    def tile_at(i):
        return i * odd + (nslot - 1 - i) * (1 - odd)

    def attend_at(i, _):
        attend(tile_at(i), 0)
        return 0

    attend_at(0, 0)
    line_forward(wo, 1, planes - 3)
    lax.fori_loop(1, nslot - 1, attend_at, 0)
    line_forward(wo, 1, planes - 2)

    def product(b, t):
        w = wo[pl.ds(pl.multiple_of(b * fb, fb), fb)]
        return lax.dot_general(attended[t], w, (((1,), (1,)), ((), ())), preferred_element_type=F32)

    dests = ((xo, mp_y), (x, mp_y), (xo, mp), (x, mp))

    def core_sum(i):
        t = tile_at(i)
        return remote(
            part_near.at[t], from_core.at[t], near_send.at[i], near_recv.at[i], region, mp_core
        )

    def far_sum(i, d):
        dx, dm = dests[d]
        t = tile_at(i)
        return remote(
            part_far.at[d, t],
            from_far.at[d, t],
            sum_send.at[d, i],
            sum_recv.at[d, i],
            plane * 2 + dx,
            dm,
        )

    def near(i):
        t = tile_at(i)
        for d, (dx, dm) in enumerate(dests):
            part_near[t, d] = product((dm + 1 - 2 * core) * 2 + dx, t).astype(BF16)
        core_sum(i).start()

    def far(i):
        t = tile_at(i)
        core_sum(i).wait_recv()
        for d, (dx, dm) in enumerate(dests[:3]):
            part_far[d, t] = (product(dm * 2 + dx, t) + from_core[t, d].astype(F32)).astype(BF16)
            far_sum(i, d).start()

    near(0)
    attend(tile_at(nslot - 1), 0)
    for i in range(1, nslot):
        near(i)
        far(i - 1)
    far(nslot - 1)

    at_m = pl.ds(pl.multiple_of(mine * fb, fb), fb)
    gate_e = mods[0, :, at_m].astype(F32)[2:3]
    gate_d = mods[1, :, at_m].astype(F32)[2:3]

    def update(i):
        t = tile_at(i)
        total = product(mine, t) + from_core[t, 3].astype(F32)
        for d in range(3):
            far_sum(i, d).wait_recv()
            total = total + from_far[d, t].astype(F32)
        gate = jnp.where(t < even, gate_e, gate_d)
        updated[t] = (feats[mine, t].astype(F32) + gate * total).astype(BF16)

    to_side = remote(
        updated.at[tile_at(0)],
        side,
        edge_send.at[0],
        edge_recv.at[0],
        region + 2 - 4 * odd,
        mp,
    )
    col = lax.broadcasted_iota(jnp.int32, (tok, fb), 0) % S
    share = jnp.zeros((tok, fb), F32)
    for k in range(W):
        share = jnp.where((col == k) | (col == S - W + k), blend_ref[k], share)
    near_cols = col < W
    far_cols = col >= S - W

    def across(i):
        t = tile_at(i)
        own = updated[t].astype(F32)
        if i > 0:
            before = updated[tile_at(i - 1)].astype(F32)
        else:
            before = side[...].astype(F32)
        if i < nslot - 1:
            after = updated[tile_at(i + 1)].astype(F32)
            has_left = has_right = True
        else:
            after = own
            has_left, has_right = odd == 1, odd == 0
        left = jnp.where(odd == 1, before, after)
        right = jnp.where(odd == 1, after, before)
        left = pltpu.roll(left, tok - (S - W), 0)
        right = pltpu.roll(right, S - W, 0)
        new = jnp.where(near_cols & has_left, (1.0 - share) * left + share * own, own)
        new = jnp.where(far_cols & has_right, (1.0 - share) * own + share * right, new)
        finished[t] = new.astype(BF16)

        @pl.when(far_up)
        def _():
            to_above(i).start()

        @pl.when(far_down)
        def _():
            to_below(i).start()

    reach = W * S
    low = pl.ds(0, reach)
    high = pl.ds(tok - reach, reach)

    def to_above(i):
        t = tile_at(i)
        return remote(
            finished.at[t, low],
            strips.at[0, t],
            strip_send.at[0, i],
            strip_recv.at[0, i],
            region - 2 * down,
            mp,
        )

    def to_below(i):
        t = tile_at(i)
        return remote(
            finished.at[t, high],
            strips.at[1, t],
            strip_send.at[1, i],
            strip_recv.at[1, i],
            region + 2 * down,
            mp,
        )

    row = lax.broadcasted_iota(jnp.int32, (reach, fb), 0) // S
    vshare = jnp.zeros((reach, fb), F32)
    for k in range(W):
        vshare = jnp.where(row == k, blend_ref[k], vshare)

    def to_owner(i):
        t = tile_at(i)
        return remote(
            finished.at[t], partner_done.at[t], last_send.at[i], last_recv.at[i], partner, mp
        )

    def downward(i):
        t = tile_at(i)

        @pl.when(far_up)
        def _():
            to_above(i).wait_send()
            to_below(i).wait_recv()
            own = finished[t, low].astype(F32)
            other = strips[1, t].astype(F32)
            finished[t, low] = ((1.0 - vshare) * other + vshare * own).astype(BF16)

        @pl.when(far_down)
        def _():
            to_below(i).wait_send()
            to_above(i).wait_recv()
            own = finished[t, high].astype(F32)
            other = strips[0, t].astype(F32)
            finished[t, high] = ((1.0 - vshare) * own + vshare * other).astype(BF16)

        to_owner(i).start()

    update(0)
    to_side.start()
    for i in range(1, nslot):
        update(i)
        if i == 1:
            to_side.wait_recv()
        across(i - 1)
        if i > 1:
            downward(i - 2)
    across(nslot - 1)
    downward(nslot - 2)
    downward(nslot - 1)

    start = x * even
    for s in range(nslot):
        got = finished[jnp.clip(start + s, 0, nslot - 1)]
        out_ref[s, :, half_m] = jnp.where(s < own_count, got, jnp.zeros_like(got))
    for i in range(nslot):
        to_owner(i).wait_recv()
    for s in range(nslot):
        got = partner_done[jnp.clip(start + s, 0, nslot - 1)]
        out_ref[s, :, half_o] = jnp.where(s < own_count, got, jnp.zeros_like(got))

    to_side.wait_send()
    for c in out_swaps:
        c.wait_send()
    for c in sends:
        c.wait_send()
    for i in range(nslot):
        to_owner(i).wait_send()
        core_sum(i).wait_send()
        for d in range(3):
            far_sum(i, d).wait_send()

    def drain(s, _):
        for kind, buf in ((0, wq), (1, wo)):
            for h in range(2):
                line_do(buf, kind, s, h, lambda c: c.wait_send())
        return 0

    lax.fori_loop(0, planes - 1, drain, 0)


def on_device(regions, tile_data, tile_counts, modulation, qkv_weight, out_weight, blend_weights):
    nslot, tok, wide = tile_data.shape
    rows, kinds, _ = qkv_weight.shape
    fb = wide // 2
    width = modulation.shape[2]
    nblock = width // fb
    planes = regions // 2
    wqkv = qkv_weight.reshape(rows, kinds * wide)
    vmem = pl.BlockSpec(memory_space=pltpu.VMEM)
    smem = pl.BlockSpec(memory_space=pltpu.SMEM)
    dma = pltpu.SemaphoreType.DMA
    return pl.pallas_call(
        functools.partial(kernel, regions),
        out_shape=jax.ShapeDtypeStruct(tile_data.shape, BF16),
        in_specs=[smem, smem, vmem, vmem, vmem, vmem],
        out_specs=vmem,
        scratch_shapes=[
            pltpu.VMEM((2, nslot, tok, fb), BF16),
            pltpu.VMEM((nblock, nslot, tok, fb), BF16),
            pltpu.VMEM((2, 16, width), BF16),
            pltpu.VMEM((rows, kinds * fb), BF16),
            pltpu.VMEM((width, kinds * fb), BF16),
            pltpu.VMEM((width, fb), BF16),
            pltpu.VMEM((nslot, tok, width), BF16),
            pltpu.VMEM((nslot, tok, fb), BF16),
            pltpu.VMEM((nslot, 4, tok, fb), BF16),
            pltpu.VMEM((3, nslot, tok, fb), BF16),
            pltpu.VMEM((nslot, 4, tok, fb), BF16),
            pltpu.VMEM((3, nslot, tok, fb), BF16),
            pltpu.VMEM((nslot, tok, fb), BF16),
            pltpu.VMEM((tok, fb), BF16),
            pltpu.VMEM((2, nslot, W * S, fb), BF16),
            pltpu.VMEM((nslot, tok, fb), BF16),
            pltpu.VMEM((nslot, tok, fb), BF16),
            dma((4,)),
            dma((4,)),
            dma((7,)),
            dma((7,)),
            dma((2, 2, planes - 1, 2)),
            dma((2, 2, planes - 1, 2)),
            dma((nslot,)),
            dma((nslot,)),
            dma((3, nslot)),
            dma((3, nslot)),
            dma((1,)),
            dma((1,)),
            dma((2, nslot)),
            dma((2, nslot)),
            dma((nslot,)),
            dma((nslot,)),
        ],
        compiler_params=pltpu.CompilerParams(
            collective_id=0, has_side_effects=True, vmem_limit_bytes=56 * 1024 * 1024
        ),
    )(tile_counts, blend_weights, tile_data, modulation, wqkv, out_weight)


def solution(mesh):
    return jax.shard_map(
        functools.partial(on_device, mesh.shape["region"]),
        mesh=mesh,
        in_specs=(
            P("region", None, "mp"),
            P(),
            P("region", None, None),
            P("region", None, "mp"),
            P("region", "mp"),
            P(),
        ),
        out_specs=P("region", None, "mp"),
        check_vma=False,
    )
```

```python
import functools
import math

import jax
import jax.numpy as jnp
from jax import lax
from jax.experimental import pallas as pl
from jax.experimental.pallas import tpu as pltpu
from jax.sharding import PartitionSpec as P

HDIM = 128
S = 16
W = 6
TCOLS = 8
MESH = pl.DeviceIdType.MESH
F32 = jnp.float32
BF16 = jnp.bfloat16


def kernel(
    regions,
    counts_ref,
    blend_ref,
    tiles_ref,
    mod_ref,
    wqkv_ref,
    wout_ref,
    out_ref,
    slots,
    feats,
    mods,
    stage,
    wq,
    wo,
    hidden,
    attended,
    part_near,
    part_far,
    from_core,
    from_far,
    updated,
    side,
    strips,
    finished,
    partner_done,
    swap_send,
    swap_recv,
    gather_send,
    gather_recv,
    line_send,
    line_recv,
    heads_send,
    heads_recv,
    near_send,
    near_recv,
    sum_send,
    sum_recv,
    edge_send,
    edge_recv,
    strip_send,
    strip_recv,
    last_send,
    last_recv,
):
    planes = regions // 2
    region = lax.axis_index("region")
    mp = lax.axis_index("mp")
    plane = region // 2
    x = region % 2
    xo = 1 - x
    partner = plane * 2 + xo
    core = mp % 2
    yy = mp // 2
    mp_core = yy * 2 + (1 - core)
    mp_y = (1 - yy) * 2 + core
    nslot, tok, wide = tiles_ref.shape
    fb = wide // 2
    rows = wqkv_ref.shape[0]
    kinds = wqkv_ref.shape[1] // wide
    down = TCOLS // nslot
    mine = mp * 2 + x
    has_up = plane > 0
    has_down = plane < planes - 1
    far_up = plane >= down
    far_down = plane < planes - down

    barrier = pltpu.get_barrier_semaphore()

    def greet(r, m):
        pl.semaphore_signal(barrier, inc=1, device_id=(r, m), device_id_type=MESH)

    greet(region, mp_core)
    greet(region, mp_y)
    greet(partner, mp)
    greet(partner, mp_y)
    for cond, step in ((has_up, -2), (has_down, 2), (far_up, -2 * down), (far_down, 2 * down)):

        @pl.when(cond)
        def _(step=step):
            greet(region + step, mp)

    arrivals = (
        4
        + has_up.astype(jnp.int32)
        + has_down.astype(jnp.int32)
        + far_up.astype(jnp.int32)
        + far_down.astype(jnp.int32)
    )
    pl.semaphore_wait(barrier, arrivals)

    def remote(src, dst, ssem, rsem, r, m):
        return pltpu.make_async_remote_copy(
            src_ref=src, dst_ref=dst, send_sem=ssem, recv_sem=rsem, device_id=(r, m), device_id_type=MESH
        )

    def block(buf, r):
        return buf.at[pl.ds(pl.multiple_of(r * rows, rows), rows)]

    def swap(i, src, dst):
        return remote(src, dst, swap_send.at[i], swap_recv.at[i], partner, mp)

    half_o = pl.ds(pl.multiple_of(xo * fb, fb), fb)
    half_m = pl.ds(pl.multiple_of(x * fb, fb), fb)

    def swaps(r, g):
        return (
            swap(0, stage, block(wq, r)),
            swap(1, tiles_ref.at[:, :, half_o], slots.at[g]),
            swap(2, mods.at[g], mods.at[g]),
        )

    out_swaps = swaps(region, x)
    in_swaps = swaps(partner, xo)
    for k in range(kinds):
        at = pl.ds(pl.multiple_of(k * wide + xo * fb, fb), fb)
        stage[:, k * fb : (k + 1) * fb] = wqkv_ref[:, at]
    out_swaps[0].start()
    for k in range(kinds):
        at = pl.ds(pl.multiple_of(k * wide + x * fb, fb), fb)
        wq[pl.ds(pl.multiple_of(region * rows, rows), rows), k * fb : (k + 1) * fb] = wqkv_ref[:, at]

    def line(buf, kind, way, s, h, q):
        ref = block(buf, 2 * q + h) if kind == 0 else block(buf, q)
        step = 2 if way == 0 else -2
        return remote(
            ref, ref, line_send.at[way, kind, s, h], line_recv.at[way, kind, s, h], region + step, mp
        )

    parts = (2, 1)

    def line_do(buf, kind, s, h, act):
        @pl.when(has_down & (plane - s >= 0))
        def _():
            act(line(buf, kind, 0, s, h, plane - s))

        @pl.when(has_up & (plane + s <= planes - 1))
        def _():
            act(line(buf, kind, 1, s, h, plane + s))

    def line_send_start(buf, kind, s, h):
        line_do(buf, kind, s, h, lambda c: c.start())

    def line_wait_recv(buf, kind, s):
        @pl.when(plane - s - 1 >= 0)
        def _():
            for h in range(parts[kind]):
                line(buf, kind, 0, s, h, plane - s - 1).wait_recv()

        @pl.when(plane + s + 1 <= planes - 1)
        def _():
            for h in range(parts[kind]):
                line(buf, kind, 1, s, h, plane + s + 1).wait_recv()

    def line_forward(buf, kind, s):
        line_wait_recv(buf, kind, s)

        @pl.when(s + 1 < planes - 1)
        def _():
            for h in range(parts[kind]):
                line_send_start(buf, kind, s + 1, h)

    line_send_start(wq, 0, 0, x)
    block(wo, plane)[...] = wout_ref[...]
    mods[x, 0:3, :] = mod_ref[0]
    slots[x] = tiles_ref[:, :, half_m]
    in_swaps[0].wait_recv()
    line_send_start(wq, 0, 0, xo)
    for c in out_swaps[1:]:
        c.start()

    in_swaps[1].wait_recv()
    even = counts_ref[2 * plane]
    own_count = counts_ref[region]
    for k in range(nslot):
        first = slots[0, k]
        second = slots[1, jnp.clip(k - even, 0, nslot - 1)]
        feats[mine, k] = jnp.where(k < even, first, second)

    def gather(i, b, r, m):
        return remote(feats.at[b], feats.at[b], gather_send.at[i], gather_recv.at[i], r, m)

    blocks = (mp * 2 + xo, mp_y * 2 + x, mp_y * 2 + xo)
    core_blocks = (mp_core * 2 + x, mp_core * 2 + xo, (3 - mp) * 2 + x, (3 - mp) * 2 + xo)
    sends = [
        gather(0, mine, partner, mp),
        gather(1, mine, region, mp_y),
        gather(2, mine, partner, mp_y),
        gather(3, mine, region, mp_core),
    ]
    for c in (sends[2], sends[0], sends[1], sends[3]):
        c.start()
    line_forward(wq, 0, 0)
    line_send_start(wo, 1, 0, 0)
    line_forward(wq, 0, 1)
    if planes > 3:
        line_forward(wo, 1, 0)
    for i in range(3):
        gather(i, blocks[i], region, mp_core).wait_recv()
        c = gather(4 + i, blocks[i], region, mp_core)
        c.start()
        sends.append(c)
    in_swaps[2].wait_recv()
    for i in range(4):
        gather(3 + i, core_blocks[i], region, mp_core).wait_recv()

    nblock = feats.shape[0]
    inv = 1.0 / (nblock * fb)
    mod_e = mods[0].astype(F32)
    mod_d = mods[1].astype(F32)

    def normalise(t, _):
        total = jnp.zeros((tok, 1), F32)
        for b in range(nblock):
            total = total + jnp.sum(feats[b, t].astype(F32), axis=1, keepdims=True)
        mean = total * inv
        total = jnp.zeros((tok, 1), F32)
        for b in range(nblock):
            c = feats[b, t].astype(F32) - mean
            total = total + jnp.sum(c * c, axis=1, keepdims=True)
        scale = lax.rsqrt(total * inv + 1e-06)
        mod = jnp.where(t < even, mod_e, mod_d)
        for b in range(nblock):
            at = slice(b * fb, (b + 1) * fb)
            c = (feats[b, t].astype(F32) - mean) * scale
            hidden[t, :, at] = (c * (1.0 + mod[1:2, at]) + mod[0:1, at]).astype(BF16)
        return 0

    lax.fori_loop(0, nslot, normalise, 0)

    def more(s, _):
        line_forward(wo, 1, s - 1)
        line_forward(wq, 0, s)
        return 0

    lax.fori_loop(2, planes - 2, more, 0)
    line_forward(wq, 0, planes - 2)

    heads = fb // HDIM

    def attend(t, _):
        outs = []
        proj = jnp.dot(hidden[t], wq[...], preferred_element_type=F32).astype(BF16)
        for h in range(heads):
            q = proj[:, h * HDIM : (h + 1) * HDIM]
            k = proj[:, fb + h * HDIM : fb + (h + 1) * HDIM]
            v = proj[:, 2 * fb + h * HDIM : 2 * fb + (h + 1) * HDIM]
            scores = lax.dot_general(q, k, (((1,), (1,)), ((), ())), preferred_element_type=F32)
            scores = scores * (1.0 / math.sqrt(HDIM))
            e = jnp.exp(scores - jnp.max(scores, axis=-1, keepdims=True))
            p = (e / jnp.sum(e, axis=-1, keepdims=True)).astype(BF16)
            outs.append(jnp.dot(p, v, preferred_element_type=F32).astype(BF16))
        attended[t, :, half_m] = jnp.concatenate(outs, axis=1)
        return 0

    odd = plane % 2

    def tile_at(i):
        return i * odd + (nslot - 1 - i) * (1 - odd)

    def share_heads(i):
        ref = attended.at[tile_at(i), :, half_m]
        return remote(ref, ref, heads_send.at[i], heads_recv.at[i], partner, mp)

    def other_heads(i):
        ref = attended.at[tile_at(i), :, half_o]
        return remote(ref, ref, heads_send.at[i], heads_recv.at[i], partner, mp)

    def attend_at(i, _):
        attend(tile_at(i), 0)
        share_heads(i).start()
        return 0

    attend_at(0, 0)
    line_forward(wo, 1, planes - 3)
    lax.fori_loop(1, nslot, attend_at, 0)
    line_forward(wo, 1, planes - 2)

    def product(m, t):
        w = wo[pl.ds(pl.multiple_of(m * fb, fb), fb)]
        return lax.dot_general(attended[t], w, (((1,), (1,)), ((), ())), preferred_element_type=F32)

    def core_sum(i):
        t = tile_at(i)
        return remote(
            part_near.at[t], from_core.at[t], near_send.at[i], near_recv.at[i], region, mp_core
        )

    def far_sum(i):
        t = tile_at(i)
        return remote(part_far.at[t], from_far.at[t], sum_send.at[i], sum_recv.at[i], region, mp_y)

    def near(i):
        t = tile_at(i)
        other_heads(i).wait_recv()
        part_near[t, 0] = product(3 - mp, t).astype(BF16)
        part_near[t, 1] = product(mp_core, t).astype(BF16)
        core_sum(i).start()

    def far(i):
        t = tile_at(i)
        core_sum(i).wait_recv()
        part_far[t] = (product(mp_y, t) + from_core[t, 0].astype(F32)).astype(BF16)
        far_sum(i).start()

    near(0)
    for i in range(1, nslot):
        near(i)
        far(i - 1)
    far(nslot - 1)

    groups = fb // rows

    def pick(lo, hi):
        if groups == 1:
            return jnp.where(x == 0, lo, hi)
        both = jnp.concatenate([lo, hi], axis=1)
        cols = [both[:, g * rows : (g + 1) * rows] for g in range(2 * groups)]
        return jnp.concatenate(
            [jnp.where(x == 0, cols[2 * g], cols[2 * g + 1]) for g in range(groups)], axis=1
        )

    def merge(own, other):
        evens = jnp.where(x == 0, own, other)
        odds = jnp.where(x == 0, other, own)
        if groups == 1:
            return jnp.concatenate([evens, odds], axis=1)
        cols = []
        for g in range(groups):
            at = slice(g * rows, (g + 1) * rows)
            cols += [evens[:, at], odds[:, at]]
        return jnp.concatenate(cols, axis=1)

    def gate_of(g):
        lo = pl.ds(pl.multiple_of(mp * 2 * fb, fb), fb)
        hi = pl.ds(pl.multiple_of(mp * 2 * fb + fb, fb), fb)
        return pick(mods[g, :, lo].astype(F32), mods[g, :, hi].astype(F32))[2:3]

    gate_e = gate_of(0)
    gate_d = gate_of(1)

    def update(i):
        t = tile_at(i)
        total = product(mp, t) + from_core[t, 1].astype(F32)
        far_sum(i).wait_recv()
        total = total + from_far[t].astype(F32)
        gate = jnp.where(t < even, gate_e, gate_d)
        if groups == 1:
            tile = feats[mine, t].astype(F32)
        else:
            tile = pick(feats[2 * mp, t].astype(F32), feats[2 * mp + 1, t].astype(F32))
        updated[t] = (tile + gate * total).astype(BF16)

    to_side = remote(
        updated.at[tile_at(0)],
        side,
        edge_send.at[0],
        edge_recv.at[0],
        region + 2 - 4 * odd,
        mp,
    )
    col = lax.broadcasted_iota(jnp.int32, (tok, fb), 0) % S
    share = jnp.zeros((tok, fb), F32)
    for k in range(W):
        share = jnp.where((col == k) | (col == S - W + k), blend_ref[k], share)
    near_cols = col < W
    far_cols = col >= S - W

    def across(i):
        t = tile_at(i)
        own = updated[t].astype(F32)
        if i > 0:
            before = updated[tile_at(i - 1)].astype(F32)
        else:
            before = side[...].astype(F32)
        if i < nslot - 1:
            after = updated[tile_at(i + 1)].astype(F32)
            has_left = has_right = True
        else:
            after = own
            has_left, has_right = odd == 1, odd == 0
        left = jnp.where(odd == 1, before, after)
        right = jnp.where(odd == 1, after, before)
        left = pltpu.roll(left, tok - (S - W), 0)
        right = pltpu.roll(right, S - W, 0)
        new = jnp.where(near_cols & has_left, (1.0 - share) * left + share * own, own)
        new = jnp.where(far_cols & has_right, (1.0 - share) * own + share * right, new)
        finished[t] = new.astype(BF16)

        @pl.when(far_up)
        def _():
            to_above(i).start()

        @pl.when(far_down)
        def _():
            to_below(i).start()

    reach = W * S
    low = pl.ds(0, reach)
    high = pl.ds(tok - reach, reach)

    def to_above(i):
        t = tile_at(i)
        return remote(
            finished.at[t, low],
            strips.at[0, t],
            strip_send.at[0, i],
            strip_recv.at[0, i],
            region - 2 * down,
            mp,
        )

    def to_below(i):
        t = tile_at(i)
        return remote(
            finished.at[t, high],
            strips.at[1, t],
            strip_send.at[1, i],
            strip_recv.at[1, i],
            region + 2 * down,
            mp,
        )

    row = lax.broadcasted_iota(jnp.int32, (reach, fb), 0) // S
    vshare = jnp.zeros((reach, fb), F32)
    for k in range(W):
        vshare = jnp.where(row == k, blend_ref[k], vshare)

    def to_owner(i):
        t = tile_at(i)
        return remote(
            finished.at[t], partner_done.at[t], last_send.at[i], last_recv.at[i], partner, mp
        )

    def downward(i):
        t = tile_at(i)

        @pl.when(far_up)
        def _():
            to_above(i).wait_send()
            to_below(i).wait_recv()
            own = finished[t, low].astype(F32)
            other = strips[1, t].astype(F32)
            finished[t, low] = ((1.0 - vshare) * other + vshare * own).astype(BF16)

        @pl.when(far_down)
        def _():
            to_below(i).wait_send()
            to_above(i).wait_recv()
            own = finished[t, high].astype(F32)
            other = strips[0, t].astype(F32)
            finished[t, high] = ((1.0 - vshare) * own + vshare * other).astype(BF16)

        to_owner(i).start()

    update(0)
    to_side.start()
    for i in range(1, nslot):
        update(i)
        if i == 1:
            to_side.wait_recv()
        across(i - 1)
        if i > 1:
            downward(i - 2)
    across(nslot - 1)
    downward(nslot - 2)
    downward(nslot - 1)

    start = x * even
    if groups == 1:
        for s in range(nslot):
            got = finished[jnp.clip(start + s, 0, nslot - 1)]
            out_ref[s, :, half_m] = jnp.where(s < own_count, got, jnp.zeros_like(got))
    for i in range(nslot):
        to_owner(i).wait_recv()
    for s in range(nslot):
        got = partner_done[jnp.clip(start + s, 0, nslot - 1)]
        if groups == 1:
            out_ref[s, :, half_o] = jnp.where(s < own_count, got, jnp.zeros_like(got))
        else:
            own = finished[jnp.clip(start + s, 0, nslot - 1)]
            got = merge(own.astype(F32), got.astype(F32)).astype(BF16)
            out_ref[s] = jnp.where(s < own_count, got, jnp.zeros_like(got))

    to_side.wait_send()
    for c in out_swaps:
        c.wait_send()
    for c in sends:
        c.wait_send()
    for i in range(nslot):
        to_owner(i).wait_send()
        core_sum(i).wait_send()
        far_sum(i).wait_send()
        share_heads(i).wait_send()

    def drain(s, _):
        for kind, buf in ((0, wq), (1, wo)):
            for h in range(parts[kind]):
                line_do(buf, kind, s, h, lambda c: c.wait_send())
        return 0

    lax.fori_loop(0, planes - 1, drain, 0)


def on_device(regions, tile_data, tile_counts, modulation, qkv_weight, out_weight, blend_weights):
    nslot, tok, wide = tile_data.shape
    rows, kinds, _ = qkv_weight.shape
    fb = wide // 2
    width = modulation.shape[2]
    nblock = width // fb
    planes = regions // 2
    wqkv = qkv_weight.reshape(rows, kinds * wide)
    vmem = pl.BlockSpec(memory_space=pltpu.VMEM)
    smem = pl.BlockSpec(memory_space=pltpu.SMEM)
    dma = pltpu.SemaphoreType.DMA
    return pl.pallas_call(
        functools.partial(kernel, regions),
        out_shape=jax.ShapeDtypeStruct(tile_data.shape, BF16),
        in_specs=[smem, smem, vmem, vmem, vmem, vmem],
        out_specs=vmem,
        scratch_shapes=[
            pltpu.VMEM((2, nslot, tok, fb), BF16),
            pltpu.VMEM((nblock, nslot, tok, fb), BF16),
            pltpu.VMEM((2, 16, width), BF16),
            pltpu.VMEM((rows, kinds * fb), BF16),
            pltpu.VMEM((width, kinds * fb), BF16),
            pltpu.VMEM((planes * rows, wide), BF16),
            pltpu.VMEM((nslot, tok, width), BF16),
            pltpu.VMEM((nslot, tok, wide), BF16),
            pltpu.VMEM((nslot, 2, tok, fb), BF16),
            pltpu.VMEM((nslot, tok, fb), BF16),
            pltpu.VMEM((nslot, 2, tok, fb), BF16),
            pltpu.VMEM((nslot, tok, fb), BF16),
            pltpu.VMEM((nslot, tok, fb), BF16),
            pltpu.VMEM((tok, fb), BF16),
            pltpu.VMEM((2, nslot, W * S, fb), BF16),
            pltpu.VMEM((nslot, tok, fb), BF16),
            pltpu.VMEM((nslot, tok, fb), BF16),
            dma((3,)),
            dma((3,)),
            dma((7,)),
            dma((7,)),
            dma((2, 2, planes - 1, 2)),
            dma((2, 2, planes - 1, 2)),
            dma((nslot,)),
            dma((nslot,)),
            dma((nslot,)),
            dma((nslot,)),
            dma((nslot,)),
            dma((nslot,)),
            dma((1,)),
            dma((1,)),
            dma((2, nslot)),
            dma((2, nslot)),
            dma((nslot,)),
            dma((nslot,)),
        ],
        compiler_params=pltpu.CompilerParams(
            collective_id=0, has_side_effects=True, vmem_limit_bytes=56 * 1024 * 1024
        ),
    )(tile_counts, blend_weights, tile_data, modulation, wqkv, out_weight)


def solution(mesh):
    return jax.shard_map(
        functools.partial(on_device, mesh.shape["region"]),
        mesh=mesh,
        in_specs=(
            P("region", None, "mp"),
            P(),
            P("region", None, None),
            P("region", None, "mp"),
            P("region", "mp"),
            P(),
        ),
        out_specs=P("region", None, "mp"),
        check_vma=False,
    )
```

```python
import functools
import math

import jax
import jax.numpy as jnp
from jax import lax
from jax.experimental import pallas as pl
from jax.experimental.pallas import tpu as pltpu
from jax.sharding import PartitionSpec as P

HDIM = 128
S = 16
W = 6
TCOLS = 8
MESH = pl.DeviceIdType.MESH
F32 = jnp.float32
BF16 = jnp.bfloat16


def kernel(
    regions,
    counts_ref,
    blend_ref,
    tiles_ref,
    mod_ref,
    wqkv_ref,
    wout_ref,
    out_ref,
    slots,
    feats,
    mods,
    stage,
    wq,
    wo,
    hidden,
    attended,
    part_near,
    part_far,
    from_core,
    from_far,
    updated,
    side,
    strips,
    finished,
    partner_done,
    swap_send,
    swap_recv,
    gather_send,
    gather_recv,
    line_send,
    line_recv,
    heads_send,
    heads_recv,
    near_send,
    near_recv,
    sum_send,
    sum_recv,
    edge_send,
    edge_recv,
    strip_send,
    strip_recv,
    last_send,
    last_recv,
):
    planes = regions // 2
    region = lax.axis_index("region")
    mp = lax.axis_index("mp")
    plane = region // 2
    x = region % 2
    xo = 1 - x
    partner = plane * 2 + xo
    core = mp % 2
    yy = mp // 2
    mp_core = yy * 2 + (1 - core)
    mp_y = (1 - yy) * 2 + core
    nslot, tok, wide = tiles_ref.shape
    fb = wide // 2
    kinds, rows = wqkv_ref.shape[:2]
    down = TCOLS // nslot
    mine = mp * 2 + x
    has_up = plane > 0
    has_down = plane < planes - 1
    far_up = plane >= down
    far_down = plane < planes - down

    barrier = pltpu.get_barrier_semaphore()

    def greet(r, m):
        pl.semaphore_signal(barrier, inc=1, device_id=(r, m), device_id_type=MESH)

    greet(region, mp_core)
    greet(region, mp_y)
    greet(partner, mp)
    greet(partner, mp_y)
    for cond, step in ((has_up, -2), (has_down, 2), (far_up, -2 * down), (far_down, 2 * down)):

        @pl.when(cond)
        def _(step=step):
            greet(region + step, mp)

    arrivals = (
        4
        + has_up.astype(jnp.int32)
        + has_down.astype(jnp.int32)
        + far_up.astype(jnp.int32)
        + far_down.astype(jnp.int32)
    )
    pl.semaphore_wait(barrier, arrivals)

    def remote(src, dst, ssem, rsem, r, m):
        return pltpu.make_async_remote_copy(
            src_ref=src, dst_ref=dst, send_sem=ssem, recv_sem=rsem, device_id=(r, m), device_id_type=MESH
        )

    def block(buf, r):
        return buf.at[pl.ds(pl.multiple_of(r * rows, rows), rows)]

    def swap(i, src, dst):
        return remote(src, dst, swap_send.at[i], swap_recv.at[i], partner, mp)

    half_o = pl.ds(pl.multiple_of(xo * fb, fb), fb)
    half_m = pl.ds(pl.multiple_of(x * fb, fb), fb)

    def swaps(r, g):
        return (
            swap(0, stage, block(wq, r)),
            swap(1, tiles_ref.at[:, :, half_o], slots.at[g]),
            swap(2, mods.at[g], mods.at[g]),
        )

    out_swaps = swaps(region, x)
    in_swaps = swaps(partner, xo)
    for k in range(kinds):
        stage[:, k * fb : (k + 1) * fb] = wqkv_ref[k, :, half_o]
    out_swaps[0].start()
    for k in range(kinds):
        wq[pl.ds(pl.multiple_of(region * rows, rows), rows), k * fb : (k + 1) * fb] = wqkv_ref[k, :, half_m]

    def line(buf, kind, way, s, h, q):
        ref = block(buf, 2 * q + h) if kind == 0 else block(buf, q)
        step = 2 if way == 0 else -2
        return remote(
            ref, ref, line_send.at[way, kind, s, h], line_recv.at[way, kind, s, h], region + step, mp
        )

    parts = (2, 1)

    def line_do(buf, kind, s, h, act):
        @pl.when(has_down & (plane - s >= 0))
        def _():
            act(line(buf, kind, 0, s, h, plane - s))

        @pl.when(has_up & (plane + s <= planes - 1))
        def _():
            act(line(buf, kind, 1, s, h, plane + s))

    def line_send_start(buf, kind, s, h):
        line_do(buf, kind, s, h, lambda c: c.start())

    def line_forward(buf, kind, s, h):
        @pl.when(plane - s - 1 >= 0)
        def _():
            line(buf, kind, 0, s, h, plane - s - 1).wait_recv()

        @pl.when(plane + s + 1 <= planes - 1)
        def _():
            line(buf, kind, 1, s, h, plane + s + 1).wait_recv()

        @pl.when(s + 1 < planes - 1)
        def _():
            line_send_start(buf, kind, s + 1, h)

    def forward_wq(s):
        line_forward(wq, 0, s, x)
        line_forward(wq, 0, s, xo)

    def forward_wo(s):
        line_forward(wo, 1, s, 0)

    line_send_start(wq, 0, 0, x)
    block(wo, plane)[...] = wout_ref[...]
    mods[x, 0:3, :] = mod_ref[0]
    slots[x] = tiles_ref[:, :, half_m]
    in_swaps[0].wait_recv()
    line_send_start(wq, 0, 0, xo)
    for c in out_swaps[1:]:
        c.start()
    line_forward(wq, 0, 0, x)

    in_swaps[1].wait_recv()
    even = counts_ref[2 * plane]
    own_count = counts_ref[region]
    for k in range(nslot):
        first = slots[0, k]
        second = slots[1, jnp.clip(k - even, 0, nslot - 1)]
        feats[mine, k] = jnp.where(k < even, first, second)

    def gather(i, b, r, m):
        return remote(feats.at[b], feats.at[b], gather_send.at[i], gather_recv.at[i], r, m)

    blocks = (mp * 2 + xo, mp_y * 2 + x, mp_y * 2 + xo)
    core_blocks = (mp_core * 2 + x, mp_core * 2 + xo, (3 - mp) * 2 + x, (3 - mp) * 2 + xo)
    sends = [
        gather(0, mine, partner, mp),
        gather(1, mine, region, mp_y),
        gather(2, mine, partner, mp_y),
        gather(3, mine, region, mp_core),
    ]
    for c in (sends[2], sends[0], sends[1], sends[3]):
        c.start()
    line_forward(wq, 0, 0, xo)
    line_send_start(wo, 1, 0, 0)
    forward_wq(1)
    forward_wo(0)
    for i in range(3):
        gather(i, blocks[i], region, mp_core).wait_recv()
        c = gather(4 + i, blocks[i], region, mp_core)
        c.start()
        sends.append(c)
    in_swaps[2].wait_recv()
    for i in range(4):
        gather(3 + i, core_blocks[i], region, mp_core).wait_recv()

    nblock = feats.shape[0]
    inv = 1.0 / (nblock * fb)
    mod_e = mods[0].astype(F32)
    mod_d = mods[1].astype(F32)

    def normalise(t, _):
        total = jnp.zeros((tok, 1), F32)
        for b in range(nblock):
            total = total + jnp.sum(feats[b, t].astype(F32), axis=1, keepdims=True)
        mean = total * inv
        total = jnp.zeros((tok, 1), F32)
        for b in range(nblock):
            c = feats[b, t].astype(F32) - mean
            total = total + jnp.sum(c * c, axis=1, keepdims=True)
        scale = lax.rsqrt(total * inv + 1e-06)
        mod = jnp.where(t < even, mod_e, mod_d)
        for b in range(nblock):
            at = slice(b * fb, (b + 1) * fb)
            c = (feats[b, t].astype(F32) - mean) * scale
            hidden[t, :, at] = (c * (1.0 + mod[1:2, at]) + mod[0:1, at]).astype(BF16)
        return 0

    lax.fori_loop(0, nslot, normalise, 0)

    def more(s, _):
        forward_wq(s)
        forward_wo(s - 1)
        return 0

    lax.fori_loop(2, planes - 2, more, 0)
    forward_wo(planes - 3)
    forward_wq(planes - 2)

    heads = fb // HDIM

    def attend(t, _):
        outs = []
        proj = jnp.dot(hidden[t], wq[...], preferred_element_type=F32).astype(BF16)
        for h in range(heads):
            q = proj[:, h * HDIM : (h + 1) * HDIM]
            k = proj[:, fb + h * HDIM : fb + (h + 1) * HDIM]
            v = proj[:, 2 * fb + h * HDIM : 2 * fb + (h + 1) * HDIM]
            scores = lax.dot_general(q, k, (((1,), (1,)), ((), ())), preferred_element_type=F32)
            scores = scores * (1.0 / math.sqrt(HDIM))
            e = jnp.exp(scores - jnp.max(scores, axis=-1, keepdims=True))
            p = (e / jnp.sum(e, axis=-1, keepdims=True)).astype(BF16)
            outs.append(jnp.dot(p, v, preferred_element_type=F32).astype(BF16))
        attended[t, :, half_m] = jnp.concatenate(outs, axis=1)
        return 0

    odd = plane % 2

    def tile_at(i):
        return i * odd + (nslot - 1 - i) * (1 - odd)

    def share_heads(i):
        ref = attended.at[tile_at(i), :, half_m]
        return remote(ref, ref, heads_send.at[i], heads_recv.at[i], partner, mp)

    def other_heads(i):
        ref = attended.at[tile_at(i), :, half_o]
        return remote(ref, ref, heads_send.at[i], heads_recv.at[i], partner, mp)

    def attend_at(i, _):
        attend(tile_at(i), 0)
        share_heads(i).start()
        return 0

    lax.fori_loop(0, nslot, attend_at, 0)
    forward_wo(planes - 2)

    def product(m, t):
        w = wo[pl.ds(pl.multiple_of(m * fb, fb), fb)]
        return lax.dot_general(attended[t], w, (((1,), (1,)), ((), ())), preferred_element_type=F32)

    def core_sum(i):
        t = tile_at(i)
        return remote(
            part_near.at[t], from_core.at[t], near_send.at[i], near_recv.at[i], region, mp_core
        )

    def far_sum(i):
        t = tile_at(i)
        return remote(part_far.at[t], from_far.at[t], sum_send.at[i], sum_recv.at[i], region, mp_y)

    def near(i):
        t = tile_at(i)
        other_heads(i).wait_recv()
        part_near[t, 0] = product(3 - mp, t).astype(BF16)
        part_near[t, 1] = product(mp_core, t).astype(BF16)
        core_sum(i).start()

    def far(i):
        t = tile_at(i)
        core_sum(i).wait_recv()
        part_far[t] = (product(mp_y, t) + from_core[t, 0].astype(F32)).astype(BF16)
        far_sum(i).start()

    near(0)
    for i in range(1, nslot):
        near(i)
        far(i - 1)
    far(nslot - 1)

    groups = fb // rows

    def pick(lo, hi):
        if groups == 1:
            return jnp.where(x == 0, lo, hi)
        both = jnp.concatenate([lo, hi], axis=1)
        cols = [both[:, g * rows : (g + 1) * rows] for g in range(2 * groups)]
        return jnp.concatenate(
            [jnp.where(x == 0, cols[2 * g], cols[2 * g + 1]) for g in range(groups)], axis=1
        )

    def merge(own, other):
        evens = jnp.where(x == 0, own, other)
        odds = jnp.where(x == 0, other, own)
        if groups == 1:
            return jnp.concatenate([evens, odds], axis=1)
        cols = []
        for g in range(groups):
            at = slice(g * rows, (g + 1) * rows)
            cols += [evens[:, at], odds[:, at]]
        return jnp.concatenate(cols, axis=1)

    def gate_of(g):
        lo = pl.ds(pl.multiple_of(mp * 2 * fb, fb), fb)
        hi = pl.ds(pl.multiple_of(mp * 2 * fb + fb, fb), fb)
        return pick(mods[g, :, lo].astype(F32), mods[g, :, hi].astype(F32))[2:3]

    gate_e = gate_of(0)
    gate_d = gate_of(1)

    def update(i):
        t = tile_at(i)
        total = product(mp, t) + from_core[t, 1].astype(F32)
        far_sum(i).wait_recv()
        total = total + from_far[t].astype(F32)
        gate = jnp.where(t < even, gate_e, gate_d)
        if groups == 1:
            tile = feats[mine, t].astype(F32)
        else:
            tile = pick(feats[2 * mp, t].astype(F32), feats[2 * mp + 1, t].astype(F32))
        updated[t] = (tile + gate * total).astype(BF16)

    to_side = remote(
        updated.at[tile_at(0)],
        side,
        edge_send.at[0],
        edge_recv.at[0],
        region + 2 - 4 * odd,
        mp,
    )
    col = lax.broadcasted_iota(jnp.int32, (tok, fb), 0) % S
    share = jnp.zeros((tok, fb), F32)
    for k in range(W):
        share = jnp.where((col == k) | (col == S - W + k), blend_ref[k], share)
    near_cols = col < W
    far_cols = col >= S - W

    def across(i):
        t = tile_at(i)
        own = updated[t].astype(F32)
        if i > 0:
            before = updated[tile_at(i - 1)].astype(F32)
        else:
            before = side[...].astype(F32)
        if i < nslot - 1:
            after = updated[tile_at(i + 1)].astype(F32)
            has_left = has_right = True
        else:
            after = own
            has_left, has_right = odd == 1, odd == 0
        left = jnp.where(odd == 1, before, after)
        right = jnp.where(odd == 1, after, before)
        left = pltpu.roll(left, tok - (S - W), 0)
        right = pltpu.roll(right, S - W, 0)
        new = jnp.where(near_cols & has_left, (1.0 - share) * left + share * own, own)
        new = jnp.where(far_cols & has_right, (1.0 - share) * own + share * right, new)
        finished[t] = new.astype(BF16)

        @pl.when(far_up)
        def _():
            to_above(i).start()

        @pl.when(far_down)
        def _():
            to_below(i).start()

    reach = W * S
    low = pl.ds(0, reach)
    high = pl.ds(tok - reach, reach)

    def to_above(i):
        t = tile_at(i)
        return remote(
            finished.at[t, low],
            strips.at[0, t],
            strip_send.at[0, i],
            strip_recv.at[0, i],
            region - 2 * down,
            mp,
        )

    def to_below(i):
        t = tile_at(i)
        return remote(
            finished.at[t, high],
            strips.at[1, t],
            strip_send.at[1, i],
            strip_recv.at[1, i],
            region + 2 * down,
            mp,
        )

    row = lax.broadcasted_iota(jnp.int32, (reach, fb), 0) // S
    vshare = jnp.zeros((reach, fb), F32)
    for k in range(W):
        vshare = jnp.where(row == k, blend_ref[k], vshare)

    def to_owner(i):
        t = tile_at(i)
        return remote(
            finished.at[t], partner_done.at[t], last_send.at[i], last_recv.at[i], partner, mp
        )

    def downward(i):
        t = tile_at(i)

        @pl.when(far_up)
        def _():
            to_above(i).wait_send()
            to_below(i).wait_recv()
            own = finished[t, low].astype(F32)
            other = strips[1, t].astype(F32)
            finished[t, low] = ((1.0 - vshare) * other + vshare * own).astype(BF16)

        @pl.when(far_down)
        def _():
            to_below(i).wait_send()
            to_above(i).wait_recv()
            own = finished[t, high].astype(F32)
            other = strips[0, t].astype(F32)
            finished[t, high] = ((1.0 - vshare) * own + vshare * other).astype(BF16)

        to_owner(i).start()

    update(0)
    to_side.start()
    for i in range(1, nslot):
        update(i)
        if i == 1:
            to_side.wait_recv()
        across(i - 1)
        if i > 1:
            downward(i - 2)
    across(nslot - 1)
    downward(nslot - 2)
    downward(nslot - 1)

    start = x * even
    if groups == 1:
        for s in range(nslot):
            got = finished[jnp.clip(start + s, 0, nslot - 1)]
            out_ref[s, :, half_m] = jnp.where(s < own_count, got, jnp.zeros_like(got))
    for i in range(nslot):
        to_owner(i).wait_recv()
    for s in range(nslot):
        got = partner_done[jnp.clip(start + s, 0, nslot - 1)]
        if groups == 1:
            out_ref[s, :, half_o] = jnp.where(s < own_count, got, jnp.zeros_like(got))
        else:
            own = finished[jnp.clip(start + s, 0, nslot - 1)]
            got = merge(own.astype(F32), got.astype(F32)).astype(BF16)
            out_ref[s] = jnp.where(s < own_count, got, jnp.zeros_like(got))

    to_side.wait_send()
    for c in out_swaps:
        c.wait_send()
    for c in sends:
        c.wait_send()
    for i in range(nslot):
        to_owner(i).wait_send()
        core_sum(i).wait_send()
        far_sum(i).wait_send()
        share_heads(i).wait_send()

    def drain(s, _):
        for kind, buf in ((0, wq), (1, wo)):
            for h in range(parts[kind]):
                line_do(buf, kind, s, h, lambda c: c.wait_send())
        return 0

    lax.fori_loop(0, planes - 1, drain, 0)


def on_device(regions, tile_data, tile_counts, modulation, qkv_weight, out_weight, blend_weights):
    nslot, tok, wide = tile_data.shape
    rows, kinds, _ = qkv_weight.shape
    fb = wide // 2
    width = modulation.shape[2]
    nblock = width // fb
    planes = regions // 2
    wqkv = qkv_weight.transpose(1, 0, 2)
    vmem = pl.BlockSpec(memory_space=pltpu.VMEM)
    smem = pl.BlockSpec(memory_space=pltpu.SMEM)
    dma = pltpu.SemaphoreType.DMA
    return pl.pallas_call(
        functools.partial(kernel, regions),
        out_shape=jax.ShapeDtypeStruct(tile_data.shape, BF16),
        in_specs=[smem, smem, vmem, vmem, vmem, vmem],
        out_specs=vmem,
        scratch_shapes=[
            pltpu.VMEM((2, nslot, tok, fb), BF16),
            pltpu.VMEM((nblock, nslot, tok, fb), BF16),
            pltpu.VMEM((2, 16, width), BF16),
            pltpu.VMEM((rows, kinds * fb), BF16),
            pltpu.VMEM((width, kinds * fb), BF16),
            pltpu.VMEM((planes * rows, wide), BF16),
            pltpu.VMEM((nslot, tok, width), BF16),
            pltpu.VMEM((nslot, tok, wide), BF16),
            pltpu.VMEM((nslot, 2, tok, fb), BF16),
            pltpu.VMEM((nslot, tok, fb), BF16),
            pltpu.VMEM((nslot, 2, tok, fb), BF16),
            pltpu.VMEM((nslot, tok, fb), BF16),
            pltpu.VMEM((nslot, tok, fb), BF16),
            pltpu.VMEM((tok, fb), BF16),
            pltpu.VMEM((2, nslot, W * S, fb), BF16),
            pltpu.VMEM((nslot, tok, fb), BF16),
            pltpu.VMEM((nslot, tok, fb), BF16),
            dma((3,)),
            dma((3,)),
            dma((7,)),
            dma((7,)),
            dma((2, 2, planes - 1, 2)),
            dma((2, 2, planes - 1, 2)),
            dma((nslot,)),
            dma((nslot,)),
            dma((nslot,)),
            dma((nslot,)),
            dma((nslot,)),
            dma((nslot,)),
            dma((1,)),
            dma((1,)),
            dma((2, nslot)),
            dma((2, nslot)),
            dma((nslot,)),
            dma((nslot,)),
        ],
        compiler_params=pltpu.CompilerParams(
            collective_id=0, has_side_effects=True, vmem_limit_bytes=56 * 1024 * 1024
        ),
    )(tile_counts, blend_weights, tile_data, modulation, wqkv, out_weight)


def solution(mesh):
    return jax.shard_map(
        functools.partial(on_device, mesh.shape["region"]),
        mesh=mesh,
        in_specs=(
            P("region", None, "mp"),
            P(),
            P("region", None, None),
            P("region", None, "mp"),
            P("region", "mp"),
            P(),
        ),
        out_specs=P("region", None, "mp"),
        check_vma=False,
    )
```

```python
import functools
import math

import jax
import jax.numpy as jnp
from jax import lax
from jax.experimental import pallas as pl
from jax.experimental.pallas import tpu as pltpu
from jax.sharding import PartitionSpec as P

HDIM = 128
S = 16
W = 6
TCOLS = 8
MESH = pl.DeviceIdType.MESH
F32 = jnp.float32
BF16 = jnp.bfloat16


def kernel(
    regions,
    counts_ref,
    blend_ref,
    tiles_ref,
    mod_ref,
    wqkv_ref,
    wout_ref,
    out_ref,
    slots,
    feats,
    mods,
    stage,
    wq,
    wo,
    hidden,
    attended,
    part_near,
    part_far,
    from_core,
    from_far,
    updated,
    side,
    strips,
    finished,
    partner_done,
    swap_send,
    swap_recv,
    gather_send,
    gather_recv,
    line_send,
    line_recv,
    heads_send,
    heads_recv,
    near_send,
    near_recv,
    sum_send,
    sum_recv,
    edge_send,
    edge_recv,
    strip_send,
    strip_recv,
    last_send,
    last_recv,
):
    planes = regions // 2
    region = lax.axis_index("region")
    mp = lax.axis_index("mp")
    plane = region // 2
    x = region % 2
    xo = 1 - x
    partner = plane * 2 + xo
    core = mp % 2
    yy = mp // 2
    mp_core = yy * 2 + (1 - core)
    mp_y = (1 - yy) * 2 + core
    nslot, tok, wide = tiles_ref.shape
    fb = wide // 2
    kinds, rows = wqkv_ref.shape[:2]
    down = TCOLS // nslot
    mine = mp * 2 + x
    has_up = plane > 0
    has_down = plane < planes - 1
    far_up = plane >= down
    far_down = plane < planes - down

    barrier = pltpu.get_barrier_semaphore()

    def greet(r, m):
        pl.semaphore_signal(barrier, inc=1, device_id=(r, m), device_id_type=MESH)

    greet(region, mp_core)
    greet(region, mp_y)
    greet(partner, mp)
    greet(partner, mp_y)
    for cond, step in ((has_up, -2), (has_down, 2), (far_up, -2 * down), (far_down, 2 * down)):

        @pl.when(cond)
        def _(step=step):
            greet(region + step, mp)

    arrivals = (
        4
        + has_up.astype(jnp.int32)
        + has_down.astype(jnp.int32)
        + far_up.astype(jnp.int32)
        + far_down.astype(jnp.int32)
    )
    half_o = pl.ds(pl.multiple_of(xo * fb, fb), fb)
    half_m = pl.ds(pl.multiple_of(x * fb, fb), fb)
    for k in range(kinds):
        at = slice(k * fb, (k + 1) * fb)
        wq[pl.ds(pl.multiple_of(region * rows, rows), rows), at] = wqkv_ref[k, :, half_m]
        stage[:, at] = wqkv_ref[k, :, half_o]
    wo[pl.ds(pl.multiple_of(plane * rows, rows), rows)] = wout_ref[...]
    pl.semaphore_wait(barrier, arrivals)

    def remote(src, dst, ssem, rsem, r, m):
        return pltpu.make_async_remote_copy(
            src_ref=src, dst_ref=dst, send_sem=ssem, recv_sem=rsem, device_id=(r, m), device_id_type=MESH
        )

    def block(buf, r):
        return buf.at[pl.ds(pl.multiple_of(r * rows, rows), rows)]

    def swap(i, src, dst):
        return remote(src, dst, swap_send.at[i], swap_recv.at[i], partner, mp)

    def swaps(r, g):
        return (
            swap(0, stage, block(wq, r)),
            swap(1, tiles_ref.at[:, :, half_o], slots.at[g]),
            swap(2, mods.at[g], mods.at[g]),
        )

    out_swaps = swaps(region, x)
    in_swaps = swaps(partner, xo)
    out_swaps[0].start()

    def line(buf, kind, way, s, h, q):
        ref = block(buf, 2 * q + h) if kind == 0 else block(buf, q)
        step = 2 if way == 0 else -2
        return remote(
            ref, ref, line_send.at[way, kind, s, h], line_recv.at[way, kind, s, h], region + step, mp
        )

    parts = (2, 1)

    def line_do(buf, kind, s, h, act):
        @pl.when(has_down & (plane - s >= 0))
        def _():
            act(line(buf, kind, 0, s, h, plane - s))

        @pl.when(has_up & (plane + s <= planes - 1))
        def _():
            act(line(buf, kind, 1, s, h, plane + s))

    def line_send_start(buf, kind, s, h):
        line_do(buf, kind, s, h, lambda c: c.start())

    def line_forward(buf, kind, s, h):
        @pl.when(plane - s - 1 >= 0)
        def _():
            line(buf, kind, 0, s, h, plane - s - 1).wait_recv()

        @pl.when(plane + s + 1 <= planes - 1)
        def _():
            line(buf, kind, 1, s, h, plane + s + 1).wait_recv()

        @pl.when(s + 1 < planes - 1)
        def _():
            line_send_start(buf, kind, s + 1, h)

    def forward_wq(s):
        line_forward(wq, 0, s, x)
        line_forward(wq, 0, s, xo)

    def forward_wo(s):
        line_forward(wo, 1, s, 0)

    line_send_start(wq, 0, 0, x)
    line_send_start(wo, 1, 0, 0)
    mods[x, 0:3, :] = mod_ref[0]
    slots[x] = tiles_ref[:, :, half_m]
    in_swaps[0].wait_recv()
    line_send_start(wq, 0, 0, xo)
    for c in out_swaps[1:]:
        c.start()
    line_forward(wq, 0, 0, x)

    in_swaps[1].wait_recv()
    even = counts_ref[2 * plane]
    own_count = counts_ref[region]
    for k in range(nslot):
        first = slots[0, k]
        second = slots[1, jnp.clip(k - even, 0, nslot - 1)]
        feats[mine, k] = jnp.where(k < even, first, second)

    def gather(i, b, r, m):
        return remote(feats.at[b], feats.at[b], gather_send.at[i], gather_recv.at[i], r, m)

    blocks = (mp * 2 + xo, mp_y * 2 + x, mp_y * 2 + xo)
    core_blocks = (mp_core * 2 + x, mp_core * 2 + xo, (3 - mp) * 2 + x, (3 - mp) * 2 + xo)
    sends = [
        gather(0, mine, partner, mp),
        gather(1, mine, region, mp_y),
        gather(2, mine, partner, mp_y),
        gather(3, mine, region, mp_core),
    ]
    for c in (sends[2], sends[0], sends[1], sends[3]):
        c.start()
    line_forward(wq, 0, 0, xo)
    forward_wq(1)
    forward_wo(0)
    for i in range(3):
        gather(i, blocks[i], region, mp_core).wait_recv()
        c = gather(4 + i, blocks[i], region, mp_core)
        c.start()
        sends.append(c)
    in_swaps[2].wait_recv()
    for i in range(4):
        gather(3 + i, core_blocks[i], region, mp_core).wait_recv()

    nblock = feats.shape[0]
    inv = 1.0 / (nblock * fb)
    mod_e = mods[0].astype(F32)
    mod_d = mods[1].astype(F32)

    def normalise(t, _):
        total = jnp.zeros((tok, 1), F32)
        for b in range(nblock):
            total = total + jnp.sum(feats[b, t].astype(F32), axis=1, keepdims=True)
        mean = total * inv
        total = jnp.zeros((tok, 1), F32)
        for b in range(nblock):
            c = feats[b, t].astype(F32) - mean
            total = total + jnp.sum(c * c, axis=1, keepdims=True)
        scale = lax.rsqrt(total * inv + 1e-06)
        mod = jnp.where(t < even, mod_e, mod_d)
        for b in range(nblock):
            at = slice(b * fb, (b + 1) * fb)
            c = (feats[b, t].astype(F32) - mean) * scale
            hidden[t, :, at] = (c * (1.0 + mod[1:2, at]) + mod[0:1, at]).astype(BF16)
        return 0

    lax.fori_loop(0, nslot, normalise, 0)

    def more(s, _):
        forward_wq(s)
        forward_wo(s - 1)
        return 0

    lax.fori_loop(2, planes - 2, more, 0)
    forward_wo(planes - 3)
    forward_wq(planes - 2)

    heads = fb // HDIM

    def attend(t, _):
        outs = []
        proj = jnp.dot(hidden[t], wq[...], preferred_element_type=F32).astype(BF16)
        for h in range(heads):
            q = proj[:, h * HDIM : (h + 1) * HDIM]
            k = proj[:, fb + h * HDIM : fb + (h + 1) * HDIM]
            v = proj[:, 2 * fb + h * HDIM : 2 * fb + (h + 1) * HDIM]
            scores = lax.dot_general(q, k, (((1,), (1,)), ((), ())), preferred_element_type=F32)
            scores = scores * (1.0 / math.sqrt(HDIM))
            e = jnp.exp(scores - jnp.max(scores, axis=-1, keepdims=True))
            p = (e / jnp.sum(e, axis=-1, keepdims=True)).astype(BF16)
            outs.append(jnp.dot(p, v, preferred_element_type=F32).astype(BF16))
        attended[t, :, half_m] = jnp.concatenate(outs, axis=1)
        return 0

    odd = plane % 2

    def tile_at(i):
        return i * odd + (nslot - 1 - i) * (1 - odd)

    def share_heads(i):
        ref = attended.at[tile_at(i), :, half_m]
        return remote(ref, ref, heads_send.at[i], heads_recv.at[i], partner, mp)

    def other_heads(i):
        ref = attended.at[tile_at(i), :, half_o]
        return remote(ref, ref, heads_send.at[i], heads_recv.at[i], partner, mp)

    def attend_at(i, _):
        attend(tile_at(i), 0)
        share_heads(i).start()
        return 0

    lax.fori_loop(0, nslot, attend_at, 0)

    def product(m, t):
        w = wo[pl.ds(pl.multiple_of(m * fb, fb), fb)]
        return lax.dot_general(attended[t], w, (((1,), (1,)), ((), ())), preferred_element_type=F32)

    def core_sum(i, j):
        t = tile_at(i)
        return remote(
            part_near.at[t, j],
            from_core.at[t, j],
            near_send.at[i, j],
            near_recv.at[i, j],
            region,
            mp_core,
        )

    def far_sum(i):
        t = tile_at(i)
        return remote(part_far.at[t], from_far.at[t], sum_send.at[i], sum_recv.at[i], region, mp_y)

    def near(i, wanted):
        t = tile_at(i)
        for j, m in ((0, 3 - mp), (1, mp_core)):

            @pl.when(wanted(m))
            def _(j=j, m=m):
                part_near[t, j] = product(m, t).astype(BF16)
                core_sum(i, j).start()

    def far(i, wanted):
        t = tile_at(i)

        @pl.when(wanted(mp_y))
        def _():
            core_sum(i, 0).wait_recv()
            part_far[t] = (product(mp_y, t) + from_core[t, 0].astype(F32)).astype(BF16)
            far_sum(i).start()

    latest = jnp.where(plane < planes // 2, 3, 0)

    def early(m):
        return m != latest

    def late(m):
        return m == latest

    for i in range(nslot):
        other_heads(i).wait_recv()
        near(i, early)
        if i > 0:
            far(i - 1, early)
    far(nslot - 1, early)
    forward_wo(planes - 2)
    for i in range(nslot):
        near(i, late)
        far(i, late)

    groups = fb // rows

    def pick(lo, hi):
        if groups == 1:
            return jnp.where(x == 0, lo, hi)
        both = jnp.concatenate([lo, hi], axis=1)
        cols = [both[:, g * rows : (g + 1) * rows] for g in range(2 * groups)]
        return jnp.concatenate(
            [jnp.where(x == 0, cols[2 * g], cols[2 * g + 1]) for g in range(groups)], axis=1
        )

    def merge(own, other):
        evens = jnp.where(x == 0, own, other)
        odds = jnp.where(x == 0, other, own)
        if groups == 1:
            return jnp.concatenate([evens, odds], axis=1)
        cols = []
        for g in range(groups):
            at = slice(g * rows, (g + 1) * rows)
            cols += [evens[:, at], odds[:, at]]
        return jnp.concatenate(cols, axis=1)

    def gate_of(g):
        lo = pl.ds(pl.multiple_of(mp * 2 * fb, fb), fb)
        hi = pl.ds(pl.multiple_of(mp * 2 * fb + fb, fb), fb)
        return pick(mods[g, :, lo].astype(F32), mods[g, :, hi].astype(F32))[2:3]

    gate_e = gate_of(0)
    gate_d = gate_of(1)

    def update(i):
        t = tile_at(i)
        total = product(mp, t)
        core_sum(i, 1).wait_recv()
        total = total + from_core[t, 1].astype(F32)
        far_sum(i).wait_recv()
        total = total + from_far[t].astype(F32)
        gate = jnp.where(t < even, gate_e, gate_d)
        if groups == 1:
            tile = feats[mine, t].astype(F32)
        else:
            tile = pick(feats[2 * mp, t].astype(F32), feats[2 * mp + 1, t].astype(F32))
        updated[t] = (tile + gate * total).astype(BF16)

    to_side = remote(
        updated.at[tile_at(0)],
        side,
        edge_send.at[0],
        edge_recv.at[0],
        region + 2 - 4 * odd,
        mp,
    )
    col = lax.broadcasted_iota(jnp.int32, (tok, fb), 0) % S
    share = jnp.zeros((tok, fb), F32)
    for k in range(W):
        share = jnp.where((col == k) | (col == S - W + k), blend_ref[k], share)
    near_cols = col < W
    far_cols = col >= S - W

    def across(i):
        t = tile_at(i)
        own = updated[t].astype(F32)
        if i > 0:
            before = updated[tile_at(i - 1)].astype(F32)
        else:
            before = side[...].astype(F32)
        if i < nslot - 1:
            after = updated[tile_at(i + 1)].astype(F32)
            has_left = has_right = True
        else:
            after = own
            has_left, has_right = odd == 1, odd == 0
        left = jnp.where(odd == 1, before, after)
        right = jnp.where(odd == 1, after, before)
        left = pltpu.roll(left, tok - (S - W), 0)
        right = pltpu.roll(right, S - W, 0)
        new = jnp.where(near_cols & has_left, (1.0 - share) * left + share * own, own)
        new = jnp.where(far_cols & has_right, (1.0 - share) * own + share * right, new)
        finished[t] = new.astype(BF16)

        @pl.when(far_up)
        def _():
            to_above(i).start()

        @pl.when(far_down)
        def _():
            to_below(i).start()

    reach = W * S
    low = pl.ds(0, reach)
    high = pl.ds(tok - reach, reach)

    def to_above(i):
        t = tile_at(i)
        return remote(
            finished.at[t, low],
            strips.at[0, t],
            strip_send.at[0, i],
            strip_recv.at[0, i],
            region - 2 * down,
            mp,
        )

    def to_below(i):
        t = tile_at(i)
        return remote(
            finished.at[t, high],
            strips.at[1, t],
            strip_send.at[1, i],
            strip_recv.at[1, i],
            region + 2 * down,
            mp,
        )

    row = lax.broadcasted_iota(jnp.int32, (reach, fb), 0) // S
    vshare = jnp.zeros((reach, fb), F32)
    for k in range(W):
        vshare = jnp.where(row == k, blend_ref[k], vshare)

    def to_owner(i):
        t = tile_at(i)
        return remote(
            finished.at[t], partner_done.at[t], last_send.at[i], last_recv.at[i], partner, mp
        )

    def downward(i):
        t = tile_at(i)

        @pl.when(far_up)
        def _():
            to_above(i).wait_send()
            to_below(i).wait_recv()
            own = finished[t, low].astype(F32)
            other = strips[1, t].astype(F32)
            finished[t, low] = ((1.0 - vshare) * other + vshare * own).astype(BF16)

        @pl.when(far_down)
        def _():
            to_below(i).wait_send()
            to_above(i).wait_recv()
            own = finished[t, high].astype(F32)
            other = strips[0, t].astype(F32)
            finished[t, high] = ((1.0 - vshare) * own + vshare * other).astype(BF16)

        to_owner(i).start()

    update(0)
    to_side.start()
    for i in range(1, nslot):
        update(i)
        if i == 1:
            to_side.wait_recv()
        across(i - 1)
        if i > 1:
            downward(i - 2)
    across(nslot - 1)
    downward(nslot - 2)
    downward(nslot - 1)

    start = x * even
    if groups == 1:
        for s in range(nslot):
            got = finished[jnp.clip(start + s, 0, nslot - 1)]
            out_ref[s, :, half_m] = jnp.where(s < own_count, got, jnp.zeros_like(got))
    for i in range(nslot):
        to_owner(i).wait_recv()
    for s in range(nslot):
        got = partner_done[jnp.clip(start + s, 0, nslot - 1)]
        if groups == 1:
            out_ref[s, :, half_o] = jnp.where(s < own_count, got, jnp.zeros_like(got))
        else:
            own = finished[jnp.clip(start + s, 0, nslot - 1)]
            got = merge(own.astype(F32), got.astype(F32)).astype(BF16)
            out_ref[s] = jnp.where(s < own_count, got, jnp.zeros_like(got))

    to_side.wait_send()
    for c in out_swaps:
        c.wait_send()
    for c in sends:
        c.wait_send()
    for i in range(nslot):
        to_owner(i).wait_send()
        core_sum(i, 0).wait_send()
        core_sum(i, 1).wait_send()
        far_sum(i).wait_send()
        share_heads(i).wait_send()

    def drain(s, _):
        for kind, buf in ((0, wq), (1, wo)):
            for h in range(parts[kind]):
                line_do(buf, kind, s, h, lambda c: c.wait_send())
        return 0

    lax.fori_loop(0, planes - 1, drain, 0)


def on_device(regions, tile_data, tile_counts, modulation, qkv_weight, out_weight, blend_weights):
    nslot, tok, wide = tile_data.shape
    rows, kinds, _ = qkv_weight.shape
    fb = wide // 2
    width = modulation.shape[2]
    nblock = width // fb
    planes = regions // 2
    wqkv = qkv_weight.transpose(1, 0, 2)
    vmem = pl.BlockSpec(memory_space=pltpu.VMEM)
    smem = pl.BlockSpec(memory_space=pltpu.SMEM)
    dma = pltpu.SemaphoreType.DMA
    return pl.pallas_call(
        functools.partial(kernel, regions),
        out_shape=jax.ShapeDtypeStruct(tile_data.shape, BF16),
        in_specs=[smem, smem, vmem, vmem, vmem, vmem],
        out_specs=vmem,
        scratch_shapes=[
            pltpu.VMEM((2, nslot, tok, fb), BF16),
            pltpu.VMEM((nblock, nslot, tok, fb), BF16),
            pltpu.VMEM((2, 16, width), BF16),
            pltpu.VMEM((rows, kinds * fb), BF16),
            pltpu.VMEM((width, kinds * fb), BF16),
            pltpu.VMEM((planes * rows, wide), BF16),
            pltpu.VMEM((nslot, tok, width), BF16),
            pltpu.VMEM((nslot, tok, wide), BF16),
            pltpu.VMEM((nslot, 2, tok, fb), BF16),
            pltpu.VMEM((nslot, tok, fb), BF16),
            pltpu.VMEM((nslot, 2, tok, fb), BF16),
            pltpu.VMEM((nslot, tok, fb), BF16),
            pltpu.VMEM((nslot, tok, fb), BF16),
            pltpu.VMEM((tok, fb), BF16),
            pltpu.VMEM((2, nslot, W * S, fb), BF16),
            pltpu.VMEM((nslot, tok, fb), BF16),
            pltpu.VMEM((nslot, tok, fb), BF16),
            dma((3,)),
            dma((3,)),
            dma((7,)),
            dma((7,)),
            dma((2, 2, planes - 1, 2)),
            dma((2, 2, planes - 1, 2)),
            dma((nslot,)),
            dma((nslot,)),
            dma((nslot, 2)),
            dma((nslot, 2)),
            dma((nslot,)),
            dma((nslot,)),
            dma((1,)),
            dma((1,)),
            dma((2, nslot)),
            dma((2, nslot)),
            dma((nslot,)),
            dma((nslot,)),
        ],
        compiler_params=pltpu.CompilerParams(
            collective_id=0, has_side_effects=True, vmem_limit_bytes=56 * 1024 * 1024
        ),
    )(tile_counts, blend_weights, tile_data, modulation, wqkv, out_weight)


def solution(mesh):
    return jax.shard_map(
        functools.partial(on_device, mesh.shape["region"]),
        mesh=mesh,
        in_specs=(
            P("region", None, "mp"),
            P(),
            P("region", None, None),
            P("region", None, "mp"),
            P("region", "mp"),
            P(),
        ),
        out_specs=P("region", None, "mp"),
        check_vma=False,
    )
```

```python
import functools
import math

import jax
import jax.numpy as jnp
from jax import lax
from jax.experimental import pallas as pl
from jax.experimental.pallas import tpu as pltpu
from jax.sharding import PartitionSpec as P

HDIM = 128
S = 16
W = 6
TCOLS = 8
MESH = pl.DeviceIdType.MESH
F32 = jnp.float32
BF16 = jnp.bfloat16


def kernel(
    regions,
    counts_ref,
    blend_ref,
    tiles_ref,
    mod_ref,
    wqkv_ref,
    wout_ref,
    out_ref,
    slots,
    feats,
    mods,
    stage,
    wq,
    wo,
    hidden,
    attended,
    part_near,
    part_far,
    from_core,
    from_far,
    updated,
    side,
    strips,
    finished,
    partner_done,
    swap_send,
    swap_recv,
    gather_send,
    gather_recv,
    line_send,
    line_recv,
    heads_send,
    heads_recv,
    near_send,
    near_recv,
    sum_send,
    sum_recv,
    edge_send,
    edge_recv,
    strip_send,
    strip_recv,
    last_send,
    last_recv,
):
    planes = regions // 2
    region = lax.axis_index("region")
    mp = lax.axis_index("mp")
    plane = region // 2
    x = region % 2
    xo = 1 - x
    partner = plane * 2 + xo
    core = mp % 2
    yy = mp // 2
    mp_core = yy * 2 + (1 - core)
    mp_y = (1 - yy) * 2 + core
    nslot, tok, wide = tiles_ref.shape
    fb = wide // 2
    kinds, rows = wqkv_ref.shape[:2]
    down = TCOLS // nslot
    mine = mp * 2 + x
    has_up = plane > 0
    has_down = plane < planes - 1
    far_up = plane >= down
    far_down = plane < planes - down

    barrier = pltpu.get_barrier_semaphore()

    def greet(r, m):
        pl.semaphore_signal(barrier, inc=1, device_id=(r, m), device_id_type=MESH)

    greet(region, mp_core)
    greet(region, mp_y)
    greet(partner, mp)
    greet(partner, mp_y)
    for cond, step in ((has_up, -2), (has_down, 2), (far_up, -2 * down), (far_down, 2 * down)):

        @pl.when(cond)
        def _(step=step):
            greet(region + step, mp)

    arrivals = (
        4
        + has_up.astype(jnp.int32)
        + has_down.astype(jnp.int32)
        + far_up.astype(jnp.int32)
        + far_down.astype(jnp.int32)
    )
    half_o = pl.ds(pl.multiple_of(xo * fb, fb), fb)
    half_m = pl.ds(pl.multiple_of(x * fb, fb), fb)
    for k in range(kinds):
        at = slice(k * fb, (k + 1) * fb)
        wq[pl.ds(pl.multiple_of(region * rows, rows), rows), at] = wqkv_ref[k, :, half_m]
        stage[:, at] = wqkv_ref[k, :, half_o]
    wo[pl.ds(pl.multiple_of(plane * rows, rows), rows)] = wout_ref[...]
    pl.semaphore_wait(barrier, arrivals)

    def remote(src, dst, ssem, rsem, r, m):
        return pltpu.make_async_remote_copy(
            src_ref=src, dst_ref=dst, send_sem=ssem, recv_sem=rsem, device_id=(r, m), device_id_type=MESH
        )

    def block(buf, r):
        return buf.at[pl.ds(pl.multiple_of(r * rows, rows), rows)]

    def swap(i, src, dst):
        return remote(src, dst, swap_send.at[i], swap_recv.at[i], partner, mp)

    def swaps(r, g):
        return (
            swap(0, stage, block(wq, r)),
            swap(1, tiles_ref.at[:, :, half_o], slots.at[g]),
            swap(2, mods.at[g], mods.at[g]),
        )

    out_swaps = swaps(region, x)
    in_swaps = swaps(partner, xo)
    out_swaps[0].start()

    def line(buf, kind, way, s, h, q):
        ref = block(buf, 2 * q + h) if kind == 0 else block(buf, q)
        step = 2 if way == 0 else -2
        return remote(
            ref, ref, line_send.at[way, kind, s, h], line_recv.at[way, kind, s, h], region + step, mp
        )

    parts = (2, 1)

    def line_do(buf, kind, s, h, act):
        @pl.when(has_down & (plane - s >= 0))
        def _():
            act(line(buf, kind, 0, s, h, plane - s))

        @pl.when(has_up & (plane + s <= planes - 1))
        def _():
            act(line(buf, kind, 1, s, h, plane + s))

    def line_send_start(buf, kind, s, h):
        line_do(buf, kind, s, h, lambda c: c.start())

    def line_forward(buf, kind, s, h):
        @pl.when(plane - s - 1 >= 0)
        def _():
            line(buf, kind, 0, s, h, plane - s - 1).wait_recv()

        @pl.when(plane + s + 1 <= planes - 1)
        def _():
            line(buf, kind, 1, s, h, plane + s + 1).wait_recv()

        @pl.when(s + 1 < planes - 1)
        def _():
            line_send_start(buf, kind, s + 1, h)

    def forward_wq(s):
        line_forward(wq, 0, s, x)
        line_forward(wq, 0, s, xo)

    def forward_wo(s):
        line_forward(wo, 1, s, 0)

    line_send_start(wq, 0, 0, x)
    mods[x, 0:3, :] = mod_ref[0]
    slots[x] = tiles_ref[:, :, half_m]
    in_swaps[0].wait_recv()
    line_send_start(wq, 0, 0, xo)
    for c in out_swaps[1:]:
        c.start()
    line_forward(wq, 0, 0, x)

    in_swaps[1].wait_recv()
    even = counts_ref[2 * plane]
    own_count = counts_ref[region]
    for k in range(nslot):
        first = slots[0, k]
        second = slots[1, jnp.clip(k - even, 0, nslot - 1)]
        feats[mine, k] = jnp.where(k < even, first, second)

    def gather(i, b, r, m):
        return remote(feats.at[b], feats.at[b], gather_send.at[i], gather_recv.at[i], r, m)

    from_x, from_y, diagonal = mp * 2 + xo, mp_y * 2 + x, mp_y * 2 + xo
    core_blocks = (mp_core * 2 + x, mp_core * 2 + xo, (3 - mp) * 2 + x, (3 - mp) * 2 + xo)
    half = nslot // 2

    def gather_half(i, b, r, m):
        ref = feats.at[b, pl.ds(i * half, half)]
        return remote(ref, ref, gather_send.at[7 + i], gather_recv.at[7 + i], r, m)

    sends = [
        gather(0, mine, partner, mp),
        gather(1, mine, region, mp_y),
        gather(3, mine, region, mp_core),
    ]
    for c in sends:
        c.start()
    line_forward(wq, 0, 0, xo)
    line_forward(wq, 0, 1, x)
    gather(0, from_x, partner, mp).wait_recv()
    gather(1, from_y, region, mp_y).wait_recv()
    passed = [
        gather_half(0, from_y, partner, mp),
        gather_half(1, from_x, region, mp_y),
        gather(4, from_x, region, mp_core),
        gather(5, from_y, region, mp_core),
    ]
    for c in passed:
        c.start()
    sends += passed
    line_forward(wq, 0, 1, xo)
    gather_half(0, diagonal, partner, mp).wait_recv()
    gather_half(1, diagonal, region, mp_y).wait_recv()
    c = gather(6, diagonal, region, mp_core)
    c.start()
    sends.append(c)
    line_send_start(wo, 1, 0, 0)
    in_swaps[2].wait_recv()
    for i in range(4):
        gather(3 + i, core_blocks[i], region, mp_core).wait_recv()

    nblock = feats.shape[0]
    inv = 1.0 / (nblock * fb)
    mod_e = mods[0].astype(F32)
    mod_d = mods[1].astype(F32)

    def normalise(t, _):
        total = jnp.zeros((tok, 1), F32)
        for b in range(nblock):
            total = total + jnp.sum(feats[b, t].astype(F32), axis=1, keepdims=True)
        mean = total * inv
        total = jnp.zeros((tok, 1), F32)
        for b in range(nblock):
            c = feats[b, t].astype(F32) - mean
            total = total + jnp.sum(c * c, axis=1, keepdims=True)
        scale = lax.rsqrt(total * inv + 1e-06)
        mod = jnp.where(t < even, mod_e, mod_d)
        for b in range(nblock):
            at = slice(b * fb, (b + 1) * fb)
            c = (feats[b, t].astype(F32) - mean) * scale
            hidden[t, :, at] = (c * (1.0 + mod[1:2, at]) + mod[0:1, at]).astype(BF16)
        return 0

    lax.fori_loop(0, nslot, normalise, 0)

    def more(s, _):
        forward_wq(s)
        forward_wo(s - 2)
        return 0

    lax.fori_loop(2, planes - 2, more, 0)
    forward_wq(planes - 2)

    heads = fb // HDIM

    def attend(t, _):
        outs = []
        proj = jnp.dot(hidden[t], wq[...], preferred_element_type=F32).astype(BF16)
        for h in range(heads):
            q = proj[:, h * HDIM : (h + 1) * HDIM]
            k = proj[:, fb + h * HDIM : fb + (h + 1) * HDIM]
            v = proj[:, 2 * fb + h * HDIM : 2 * fb + (h + 1) * HDIM]
            scores = lax.dot_general(q, k, (((1,), (1,)), ((), ())), preferred_element_type=F32)
            scores = scores * (1.0 / math.sqrt(HDIM))
            e = jnp.exp(scores - jnp.max(scores, axis=-1, keepdims=True))
            p = (e / jnp.sum(e, axis=-1, keepdims=True)).astype(BF16)
            outs.append(jnp.dot(p, v, preferred_element_type=F32).astype(BF16))
        attended[t, :, half_m] = jnp.concatenate(outs, axis=1)
        return 0

    odd = plane % 2

    def tile_at(i):
        return i * odd + (nslot - 1 - i) * (1 - odd)

    def share_heads(i):
        ref = attended.at[tile_at(i), :, half_m]
        return remote(ref, ref, heads_send.at[i], heads_recv.at[i], partner, mp)

    def other_heads(i):
        ref = attended.at[tile_at(i), :, half_o]
        return remote(ref, ref, heads_send.at[i], heads_recv.at[i], partner, mp)

    def attend_at(i, _):
        attend(tile_at(i), 0)
        share_heads(i).start()
        return 0

    attend_at(0, 0)
    forward_wo(planes - 4)
    attend_at(1, 0)
    forward_wo(planes - 3)
    lax.fori_loop(2, nslot, attend_at, 0)

    def product(m, t):
        w = wo[pl.ds(pl.multiple_of(m * fb, fb), fb)]
        return lax.dot_general(attended[t], w, (((1,), (1,)), ((), ())), preferred_element_type=F32)

    def core_sum(i, j):
        t = tile_at(i)
        return remote(
            part_near.at[t, j],
            from_core.at[t, j],
            near_send.at[i, j],
            near_recv.at[i, j],
            region,
            mp_core,
        )

    def far_sum(i):
        t = tile_at(i)
        return remote(part_far.at[t], from_far.at[t], sum_send.at[i], sum_recv.at[i], region, mp_y)

    def near(i, wanted):
        t = tile_at(i)
        for j, m in ((0, 3 - mp), (1, mp_core)):

            @pl.when(wanted(m))
            def _(j=j, m=m):
                part_near[t, j] = product(m, t).astype(BF16)
                core_sum(i, j).start()

    def far(i, wanted):
        t = tile_at(i)

        @pl.when(wanted(mp_y))
        def _():
            core_sum(i, 0).wait_recv()
            part_far[t] = (product(mp_y, t) + from_core[t, 0].astype(F32)).astype(BF16)
            far_sum(i).start()

    latest = jnp.where(plane < planes // 2, 3, 0)

    def early(m):
        return m != latest

    def late(m):
        return m == latest

    for i in range(nslot):
        other_heads(i).wait_recv()
        near(i, early)
        if i > 0:
            far(i - 1, early)
    far(nslot - 1, early)
    forward_wo(planes - 2)
    for i in range(nslot):
        near(i, late)
        far(i, late)

    groups = fb // rows

    def pick(lo, hi):
        if groups == 1:
            return jnp.where(x == 0, lo, hi)
        both = jnp.concatenate([lo, hi], axis=1)
        cols = [both[:, g * rows : (g + 1) * rows] for g in range(2 * groups)]
        return jnp.concatenate(
            [jnp.where(x == 0, cols[2 * g], cols[2 * g + 1]) for g in range(groups)], axis=1
        )

    def merge(own, other):
        evens = jnp.where(x == 0, own, other)
        odds = jnp.where(x == 0, other, own)
        if groups == 1:
            return jnp.concatenate([evens, odds], axis=1)
        cols = []
        for g in range(groups):
            at = slice(g * rows, (g + 1) * rows)
            cols += [evens[:, at], odds[:, at]]
        return jnp.concatenate(cols, axis=1)

    def gate_of(g):
        lo = pl.ds(pl.multiple_of(mp * 2 * fb, fb), fb)
        hi = pl.ds(pl.multiple_of(mp * 2 * fb + fb, fb), fb)
        return pick(mods[g, :, lo].astype(F32), mods[g, :, hi].astype(F32))[2:3]

    gate_e = gate_of(0)
    gate_d = gate_of(1)

    def update(i):
        t = tile_at(i)
        total = product(mp, t)
        core_sum(i, 1).wait_recv()
        total = total + from_core[t, 1].astype(F32)
        far_sum(i).wait_recv()
        total = total + from_far[t].astype(F32)
        gate = jnp.where(t < even, gate_e, gate_d)
        if groups == 1:
            tile = feats[mine, t].astype(F32)
        else:
            tile = pick(feats[2 * mp, t].astype(F32), feats[2 * mp + 1, t].astype(F32))
        updated[t] = (tile + gate * total).astype(BF16)

    to_side = remote(
        updated.at[tile_at(0)],
        side,
        edge_send.at[0],
        edge_recv.at[0],
        region + 2 - 4 * odd,
        mp,
    )
    col = lax.broadcasted_iota(jnp.int32, (tok, fb), 0) % S
    share = jnp.zeros((tok, fb), F32)
    for k in range(W):
        share = jnp.where((col == k) | (col == S - W + k), blend_ref[k], share)
    near_cols = col < W
    far_cols = col >= S - W

    def across(i):
        t = tile_at(i)
        own = updated[t].astype(F32)
        if i > 0:
            before = updated[tile_at(i - 1)].astype(F32)
        else:
            before = side[...].astype(F32)
        if i < nslot - 1:
            after = updated[tile_at(i + 1)].astype(F32)
            has_left = has_right = True
        else:
            after = own
            has_left, has_right = odd == 1, odd == 0
        left = jnp.where(odd == 1, before, after)
        right = jnp.where(odd == 1, after, before)
        left = pltpu.roll(left, tok - (S - W), 0)
        right = pltpu.roll(right, S - W, 0)
        new = jnp.where(near_cols & has_left, (1.0 - share) * left + share * own, own)
        new = jnp.where(far_cols & has_right, (1.0 - share) * own + share * right, new)
        finished[t] = new.astype(BF16)

        @pl.when(far_up)
        def _():
            to_above(i).start()

        @pl.when(far_down)
        def _():
            to_below(i).start()

    reach = W * S
    low = pl.ds(0, reach)
    high = pl.ds(tok - reach, reach)

    def to_above(i):
        t = tile_at(i)
        return remote(
            finished.at[t, low],
            strips.at[0, t],
            strip_send.at[0, i],
            strip_recv.at[0, i],
            region - 2 * down,
            mp,
        )

    def to_below(i):
        t = tile_at(i)
        return remote(
            finished.at[t, high],
            strips.at[1, t],
            strip_send.at[1, i],
            strip_recv.at[1, i],
            region + 2 * down,
            mp,
        )

    row = lax.broadcasted_iota(jnp.int32, (reach, fb), 0) // S
    vshare = jnp.zeros((reach, fb), F32)
    for k in range(W):
        vshare = jnp.where(row == k, blend_ref[k], vshare)

    def to_owner(i):
        t = tile_at(i)
        return remote(
            finished.at[t], partner_done.at[t], last_send.at[i], last_recv.at[i], partner, mp
        )

    def downward(i):
        t = tile_at(i)

        @pl.when(far_up)
        def _():
            to_above(i).wait_send()
            to_below(i).wait_recv()
            own = finished[t, low].astype(F32)
            other = strips[1, t].astype(F32)
            finished[t, low] = ((1.0 - vshare) * other + vshare * own).astype(BF16)

        @pl.when(far_down)
        def _():
            to_below(i).wait_send()
            to_above(i).wait_recv()
            own = finished[t, high].astype(F32)
            other = strips[0, t].astype(F32)
            finished[t, high] = ((1.0 - vshare) * own + vshare * other).astype(BF16)

        to_owner(i).start()

    update(0)
    to_side.start()
    for i in range(1, nslot):
        update(i)
        if i == 1:
            to_side.wait_recv()
        across(i - 1)
        if i > 1:
            downward(i - 2)
    across(nslot - 1)
    downward(nslot - 2)
    downward(nslot - 1)

    start = x * even
    if groups == 1:
        for s in range(nslot):
            got = finished[jnp.clip(start + s, 0, nslot - 1)]
            out_ref[s, :, half_m] = jnp.where(s < own_count, got, jnp.zeros_like(got))
    for i in range(nslot):
        to_owner(i).wait_recv()
    for s in range(nslot):
        got = partner_done[jnp.clip(start + s, 0, nslot - 1)]
        if groups == 1:
            out_ref[s, :, half_o] = jnp.where(s < own_count, got, jnp.zeros_like(got))
        else:
            own = finished[jnp.clip(start + s, 0, nslot - 1)]
            got = merge(own.astype(F32), got.astype(F32)).astype(BF16)
            out_ref[s] = jnp.where(s < own_count, got, jnp.zeros_like(got))

    to_side.wait_send()
    for c in out_swaps:
        c.wait_send()
    for c in sends:
        c.wait_send()
    for i in range(nslot):
        to_owner(i).wait_send()
        core_sum(i, 0).wait_send()
        core_sum(i, 1).wait_send()
        far_sum(i).wait_send()
        share_heads(i).wait_send()

    def drain(s, _):
        for kind, buf in ((0, wq), (1, wo)):
            for h in range(parts[kind]):
                line_do(buf, kind, s, h, lambda c: c.wait_send())
        return 0

    lax.fori_loop(0, planes - 1, drain, 0)


def on_device(regions, tile_data, tile_counts, modulation, qkv_weight, out_weight, blend_weights):
    nslot, tok, wide = tile_data.shape
    rows, kinds, _ = qkv_weight.shape
    fb = wide // 2
    width = modulation.shape[2]
    nblock = width // fb
    planes = regions // 2
    wqkv = qkv_weight.transpose(1, 0, 2)
    vmem = pl.BlockSpec(memory_space=pltpu.VMEM)
    smem = pl.BlockSpec(memory_space=pltpu.SMEM)
    dma = pltpu.SemaphoreType.DMA
    return pl.pallas_call(
        functools.partial(kernel, regions),
        out_shape=jax.ShapeDtypeStruct(tile_data.shape, BF16),
        in_specs=[smem, smem, vmem, vmem, vmem, vmem],
        out_specs=vmem,
        scratch_shapes=[
            pltpu.VMEM((2, nslot, tok, fb), BF16),
            pltpu.VMEM((nblock, nslot, tok, fb), BF16),
            pltpu.VMEM((2, 16, width), BF16),
            pltpu.VMEM((rows, kinds * fb), BF16),
            pltpu.VMEM((width, kinds * fb), BF16),
            pltpu.VMEM((planes * rows, wide), BF16),
            pltpu.VMEM((nslot, tok, width), BF16),
            pltpu.VMEM((nslot, tok, wide), BF16),
            pltpu.VMEM((nslot, 2, tok, fb), BF16),
            pltpu.VMEM((nslot, tok, fb), BF16),
            pltpu.VMEM((nslot, 2, tok, fb), BF16),
            pltpu.VMEM((nslot, tok, fb), BF16),
            pltpu.VMEM((nslot, tok, fb), BF16),
            pltpu.VMEM((tok, fb), BF16),
            pltpu.VMEM((2, nslot, W * S, fb), BF16),
            pltpu.VMEM((nslot, tok, fb), BF16),
            pltpu.VMEM((nslot, tok, fb), BF16),
            dma((3,)),
            dma((3,)),
            dma((9,)),
            dma((9,)),
            dma((2, 2, planes - 1, 2)),
            dma((2, 2, planes - 1, 2)),
            dma((nslot,)),
            dma((nslot,)),
            dma((nslot, 2)),
            dma((nslot, 2)),
            dma((nslot,)),
            dma((nslot,)),
            dma((1,)),
            dma((1,)),
            dma((2, nslot)),
            dma((2, nslot)),
            dma((nslot,)),
            dma((nslot,)),
        ],
        compiler_params=pltpu.CompilerParams(
            collective_id=0, has_side_effects=True, vmem_limit_bytes=56 * 1024 * 1024
        ),
    )(tile_counts, blend_weights, tile_data, modulation, wqkv, out_weight)


def solution(mesh):
    return jax.shard_map(
        functools.partial(on_device, mesh.shape["region"]),
        mesh=mesh,
        in_specs=(
            P("region", None, "mp"),
            P(),
            P("region", None, None),
            P("region", None, "mp"),
            P("region", "mp"),
            P(),
        ),
        out_specs=P("region", None, "mp"),
        check_vma=False,
    )
```

```python
import functools
import math

import jax
import jax.numpy as jnp
from jax import lax
from jax.experimental import pallas as pl
from jax.experimental.pallas import tpu as pltpu
from jax.sharding import PartitionSpec as P

HDIM = 128
S = 16
W = 6
TCOLS = 8
MESH = pl.DeviceIdType.MESH
F32 = jnp.float32
BF16 = jnp.bfloat16


def kernel(
    regions,
    counts_ref,
    blend_ref,
    tiles_ref,
    mod_ref,
    wqkv_ref,
    wout_ref,
    out_ref,
    slots,
    feats,
    mods,
    stage,
    wq,
    wo,
    hidden,
    partial,
    attended,
    part_near,
    part_far,
    from_core,
    from_far,
    updated,
    side,
    strips,
    finished,
    partner_done,
    swap_send,
    swap_recv,
    gather_send,
    gather_recv,
    line_send,
    line_recv,
    heads_send,
    heads_recv,
    near_send,
    near_recv,
    sum_send,
    sum_recv,
    edge_send,
    edge_recv,
    strip_send,
    strip_recv,
    last_send,
    last_recv,
):
    planes = regions // 2
    region = lax.axis_index("region")
    mp = lax.axis_index("mp")
    plane = region // 2
    x = region % 2
    xo = 1 - x
    partner = plane * 2 + xo
    core = mp % 2
    yy = mp // 2
    mp_core = yy * 2 + (1 - core)
    mp_y = (1 - yy) * 2 + core
    nslot, tok, wide = tiles_ref.shape
    fb = wide // 2
    kinds, rows = wqkv_ref.shape[:2]
    down = TCOLS // nslot
    mine = mp * 2 + x
    has_up = plane > 0
    has_down = plane < planes - 1
    far_up = plane >= down
    far_down = plane < planes - down

    barrier = pltpu.get_barrier_semaphore()

    def greet(r, m):
        pl.semaphore_signal(barrier, inc=1, device_id=(r, m), device_id_type=MESH)

    greet(region, mp_core)
    greet(region, mp_y)
    greet(partner, mp)
    greet(partner, mp_y)
    for cond, step in ((has_up, -2), (has_down, 2), (far_up, -2 * down), (far_down, 2 * down)):

        @pl.when(cond)
        def _(step=step):
            greet(region + step, mp)

    arrivals = (
        4
        + has_up.astype(jnp.int32)
        + has_down.astype(jnp.int32)
        + far_up.astype(jnp.int32)
        + far_down.astype(jnp.int32)
    )
    half_o = pl.ds(pl.multiple_of(xo * fb, fb), fb)
    half_m = pl.ds(pl.multiple_of(x * fb, fb), fb)
    for k in range(kinds):
        at = slice(k * fb, (k + 1) * fb)
        wq[pl.ds(pl.multiple_of(region * rows, rows), rows), at] = wqkv_ref[k, :, half_m]
        stage[:, at] = wqkv_ref[k, :, half_o]
    wo[pl.ds(pl.multiple_of(plane * rows, rows), rows)] = wout_ref[...]
    pl.semaphore_wait(barrier, arrivals)

    def remote(src, dst, ssem, rsem, r, m):
        return pltpu.make_async_remote_copy(
            src_ref=src, dst_ref=dst, send_sem=ssem, recv_sem=rsem, device_id=(r, m), device_id_type=MESH
        )

    def block(buf, r):
        return buf.at[pl.ds(pl.multiple_of(r * rows, rows), rows)]

    def swap(i, src, dst):
        return remote(src, dst, swap_send.at[i], swap_recv.at[i], partner, mp)

    def swaps(r, g):
        return (
            swap(0, stage, block(wq, r)),
            swap(1, tiles_ref.at[:, :, half_o], slots.at[g]),
            swap(2, mods.at[g], mods.at[g]),
        )

    out_swaps = swaps(region, x)
    in_swaps = swaps(partner, xo)
    out_swaps[0].start()

    def line(buf, kind, way, s, h, q):
        ref = block(buf, 2 * q + h) if kind == 0 else block(buf, q)
        step = 2 if way == 0 else -2
        return remote(
            ref, ref, line_send.at[way, kind, s, h], line_recv.at[way, kind, s, h], region + step, mp
        )

    parts = (2, 1)

    def line_do(buf, kind, s, h, act):
        @pl.when(has_down & (plane - s >= 0))
        def _():
            act(line(buf, kind, 0, s, h, plane - s))

        @pl.when(has_up & (plane + s <= planes - 1))
        def _():
            act(line(buf, kind, 1, s, h, plane + s))

    def line_send_start(buf, kind, s, h):
        line_do(buf, kind, s, h, lambda c: c.start())

    def line_forward(buf, kind, s, h):
        @pl.when(plane - s - 1 >= 0)
        def _():
            line(buf, kind, 0, s, h, plane - s - 1).wait_recv()

        @pl.when(plane + s + 1 <= planes - 1)
        def _():
            line(buf, kind, 1, s, h, plane + s + 1).wait_recv()

        @pl.when(s + 1 < planes - 1)
        def _():
            line_send_start(buf, kind, s + 1, h)

    def forward_wq(s):
        line_forward(wq, 0, s, x)
        line_forward(wq, 0, s, xo)

    def forward_wo(s):
        line_forward(wo, 1, s, 0)

    line_send_start(wq, 0, 0, x)
    mods[x, 0:3, :] = mod_ref[0]
    slots[x] = tiles_ref[:, :, half_m]
    in_swaps[0].wait_recv()
    line_send_start(wq, 0, 0, xo)
    for c in out_swaps[1:]:
        c.start()
    line_forward(wq, 0, 0, x)

    in_swaps[1].wait_recv()
    even = counts_ref[2 * plane]
    own_count = counts_ref[region]
    for k in range(nslot):
        first = slots[0, k]
        second = slots[1, jnp.clip(k - even, 0, nslot - 1)]
        feats[mine, k] = jnp.where(k < even, first, second)

    def gather(i, b, r, m):
        return remote(feats.at[b], feats.at[b], gather_send.at[i], gather_recv.at[i], r, m)

    from_x, from_y, diagonal = mp * 2 + xo, mp_y * 2 + x, mp_y * 2 + xo
    core_blocks = (mp_core * 2 + x, mp_core * 2 + xo, (3 - mp) * 2 + x, (3 - mp) * 2 + xo)
    half = nslot // 2

    def gather_half(i, b, r, m):
        ref = feats.at[b, pl.ds(i * half, half)]
        return remote(ref, ref, gather_send.at[7 + i], gather_recv.at[7 + i], r, m)

    sends = [
        gather(0, mine, partner, mp),
        gather(1, mine, region, mp_y),
        gather(3, mine, region, mp_core),
    ]
    for c in sends:
        c.start()
    line_forward(wq, 0, 0, xo)
    line_forward(wq, 0, 1, x)
    gather(0, from_x, partner, mp).wait_recv()
    gather(1, from_y, region, mp_y).wait_recv()
    passed = [
        gather_half(0, from_y, partner, mp),
        gather_half(1, from_x, region, mp_y),
        gather(4, from_x, region, mp_core),
        gather(5, from_y, region, mp_core),
    ]
    for c in passed:
        c.start()
    sends += passed
    line_forward(wq, 0, 1, xo)
    gather_half(0, diagonal, partner, mp).wait_recv()
    gather_half(1, diagonal, region, mp_y).wait_recv()
    c = gather(6, diagonal, region, mp_core)
    c.start()
    sends.append(c)
    line_send_start(wo, 1, 0, 0)
    in_swaps[2].wait_recv()
    for i in range(4):
        gather(3 + i, core_blocks[i], region, mp_core).wait_recv()

    nblock = feats.shape[0]
    inv = 1.0 / (nblock * fb)
    shift_e, gain_e = mods[0].astype(F32)[0:1], 1.0 + mods[0].astype(F32)[1:2]
    shift_d, gain_d = mods[1].astype(F32)[0:1], 1.0 + mods[1].astype(F32)[1:2]
    lines = 64
    chunks = tok // lines

    def normalise(i, _):
        t = i // chunks
        at_rows = pl.ds(pl.multiple_of((i % chunks) * lines, lines), lines)
        total = feats[0, t, at_rows].astype(F32)
        for b in range(1, nblock):
            total = total + feats[b, t, at_rows].astype(F32)
        mean = jnp.sum(total, axis=1, keepdims=True) * inv
        total = jnp.zeros((lines, fb), F32)
        for b in range(nblock):
            c = feats[b, t, at_rows].astype(F32) - mean
            total = total + c * c
        scale = lax.rsqrt(jnp.sum(total, axis=1, keepdims=True) * inv + 1e-06)
        shift = jnp.where(t < even, shift_e, shift_d)
        gain = jnp.where(t < even, gain_e, gain_d)
        for b in range(nblock):
            at = slice(b * fb, (b + 1) * fb)
            c = (feats[b, t, at_rows].astype(F32) - mean) * scale
            hidden[t, at_rows, at] = (c * gain[:, at] + shift[:, at]).astype(BF16)
        return 0

    lax.fori_loop(0, nslot * chunks, normalise, 0)

    latest = jnp.where(plane < planes // 2, 3, 0)
    group = feats.shape[0] * fb // 4

    def multiply(t, g):
        at = pl.ds(pl.multiple_of(g * group, group), group)
        return jnp.dot(hidden[t, :, at], wq[at], preferred_element_type=F32)

    def begin(t, _):
        total = multiply(t, (latest + 1) % 4) + multiply(t, (latest + 2) % 4)
        partial[t] = total + multiply(t, (latest + 3) % 4)
        return 0

    def more(s, _):
        forward_wq(s)
        forward_wo(s - 2)
        return 0

    lax.fori_loop(2, planes - 2, more, 0)
    lax.fori_loop(0, nslot, begin, 0)
    forward_wq(planes - 2)

    heads = fb // HDIM

    def attend(t, _):
        outs = []
        proj = (partial[t] + multiply(t, latest)).astype(BF16)
        for h in range(heads):
            q = proj[:, h * HDIM : (h + 1) * HDIM]
            k = proj[:, fb + h * HDIM : fb + (h + 1) * HDIM]
            v = proj[:, 2 * fb + h * HDIM : 2 * fb + (h + 1) * HDIM]
            scores = lax.dot_general(q, k, (((1,), (1,)), ((), ())), preferred_element_type=F32)
            e = jnp.exp((scores - jnp.max(scores, axis=-1, keepdims=True)) * (1.0 / math.sqrt(HDIM)))
            p = (e * (1.0 / jnp.sum(e, axis=-1, keepdims=True))).astype(BF16)
            outs.append(jnp.dot(p, v, preferred_element_type=F32).astype(BF16))
        attended[t, :, half_m] = jnp.concatenate(outs, axis=1)
        return 0

    odd = plane % 2

    def tile_at(i):
        return i * odd + (nslot - 1 - i) * (1 - odd)

    def share_heads(i):
        ref = attended.at[tile_at(i), :, half_m]
        return remote(ref, ref, heads_send.at[i], heads_recv.at[i], partner, mp)

    def other_heads(i):
        ref = attended.at[tile_at(i), :, half_o]
        return remote(ref, ref, heads_send.at[i], heads_recv.at[i], partner, mp)

    def attend_at(i, _):
        attend(tile_at(i), 0)
        share_heads(i).start()
        return 0

    attend_at(0, 0)
    forward_wo(planes - 4)
    attend_at(1, 0)
    forward_wo(planes - 3)
    lax.fori_loop(2, nslot, attend_at, 0)

    def product(m, t):
        w = wo[pl.ds(pl.multiple_of(m * fb, fb), fb)]
        return lax.dot_general(attended[t], w, (((1,), (1,)), ((), ())), preferred_element_type=F32)

    def core_sum(i, j):
        t = tile_at(i)
        return remote(
            part_near.at[t, j],
            from_core.at[t, j],
            near_send.at[i, j],
            near_recv.at[i, j],
            region,
            mp_core,
        )

    def far_sum(i):
        t = tile_at(i)
        return remote(part_far.at[t], from_far.at[t], sum_send.at[i], sum_recv.at[i], region, mp_y)

    def near(i, wanted):
        t = tile_at(i)
        for j, m in ((0, 3 - mp), (1, mp_core)):

            @pl.when(wanted(m))
            def _(j=j, m=m):
                part_near[t, j] = product(m, t).astype(BF16)
                core_sum(i, j).start()

    def far(i, wanted):
        t = tile_at(i)

        @pl.when(wanted(mp_y))
        def _():
            core_sum(i, 0).wait_recv()
            part_far[t] = (product(mp_y, t) + from_core[t, 0].astype(F32)).astype(BF16)
            far_sum(i).start()

    def early(m):
        return m != latest

    def late(m):
        return m == latest

    for i in range(nslot):
        other_heads(i).wait_recv()
        near(i, early)
        if i > 0:
            far(i - 1, early)
    far(nslot - 1, early)
    forward_wo(planes - 2)
    for i in range(nslot):
        near(i, late)
        far(i, late)

    groups = fb // rows

    def pick(lo, hi):
        if groups == 1:
            return jnp.where(x == 0, lo, hi)
        both = jnp.concatenate([lo, hi], axis=1)
        cols = [both[:, g * rows : (g + 1) * rows] for g in range(2 * groups)]
        return jnp.concatenate(
            [jnp.where(x == 0, cols[2 * g], cols[2 * g + 1]) for g in range(groups)], axis=1
        )

    def merge(own, other):
        evens = jnp.where(x == 0, own, other)
        odds = jnp.where(x == 0, other, own)
        if groups == 1:
            return jnp.concatenate([evens, odds], axis=1)
        cols = []
        for g in range(groups):
            at = slice(g * rows, (g + 1) * rows)
            cols += [evens[:, at], odds[:, at]]
        return jnp.concatenate(cols, axis=1)

    def gate_of(g):
        lo = pl.ds(pl.multiple_of(mp * 2 * fb, fb), fb)
        hi = pl.ds(pl.multiple_of(mp * 2 * fb + fb, fb), fb)
        return pick(mods[g, :, lo].astype(F32), mods[g, :, hi].astype(F32))[2:3]

    gate_e = gate_of(0)
    gate_d = gate_of(1)

    def update(i):
        t = tile_at(i)
        total = product(mp, t)
        core_sum(i, 1).wait_recv()
        total = total + from_core[t, 1].astype(F32)
        far_sum(i).wait_recv()
        total = total + from_far[t].astype(F32)
        gate = jnp.where(t < even, gate_e, gate_d)
        if groups == 1:
            tile = feats[mine, t].astype(F32)
        else:
            tile = pick(feats[2 * mp, t].astype(F32), feats[2 * mp + 1, t].astype(F32))
        updated[t] = (tile + gate * total).astype(BF16)

    to_side = remote(
        updated.at[tile_at(0)],
        side,
        edge_send.at[0],
        edge_recv.at[0],
        region + 2 - 4 * odd,
        mp,
    )
    col = lax.broadcasted_iota(jnp.int32, (tok, fb), 0) % S
    share = jnp.zeros((tok, fb), F32)
    for k in range(W):
        share = jnp.where((col == k) | (col == S - W + k), blend_ref[k], share)
    near_cols = col < W
    far_cols = col >= S - W

    def across(i):
        t = tile_at(i)
        own = updated[t].astype(F32)
        if i > 0:
            before = updated[tile_at(i - 1)].astype(F32)
        else:
            before = side[...].astype(F32)
        if i < nslot - 1:
            after = updated[tile_at(i + 1)].astype(F32)
            has_left = has_right = True
        else:
            after = own
            has_left, has_right = odd == 1, odd == 0
        left = jnp.where(odd == 1, before, after)
        right = jnp.where(odd == 1, after, before)
        left = pltpu.roll(left, tok - (S - W), 0)
        right = pltpu.roll(right, S - W, 0)
        new = jnp.where(near_cols & has_left, (1.0 - share) * left + share * own, own)
        new = jnp.where(far_cols & has_right, (1.0 - share) * own + share * right, new)
        finished[t] = new.astype(BF16)

        @pl.when(far_up)
        def _():
            to_above(i).start()

        @pl.when(far_down)
        def _():
            to_below(i).start()

    reach = W * S
    low = pl.ds(0, reach)
    high = pl.ds(tok - reach, reach)

    def to_above(i):
        t = tile_at(i)
        return remote(
            finished.at[t, low],
            strips.at[0, t],
            strip_send.at[0, i],
            strip_recv.at[0, i],
            region - 2 * down,
            mp,
        )

    def to_below(i):
        t = tile_at(i)
        return remote(
            finished.at[t, high],
            strips.at[1, t],
            strip_send.at[1, i],
            strip_recv.at[1, i],
            region + 2 * down,
            mp,
        )

    row = lax.broadcasted_iota(jnp.int32, (reach, fb), 0) // S
    vshare = jnp.zeros((reach, fb), F32)
    for k in range(W):
        vshare = jnp.where(row == k, blend_ref[k], vshare)

    def to_owner(i):
        t = tile_at(i)
        return remote(
            finished.at[t], partner_done.at[t], last_send.at[i], last_recv.at[i], partner, mp
        )

    def downward(i):
        t = tile_at(i)

        @pl.when(far_up)
        def _():
            to_above(i).wait_send()
            to_below(i).wait_recv()
            own = finished[t, low].astype(F32)
            other = strips[1, t].astype(F32)
            finished[t, low] = ((1.0 - vshare) * other + vshare * own).astype(BF16)

        @pl.when(far_down)
        def _():
            to_below(i).wait_send()
            to_above(i).wait_recv()
            own = finished[t, high].astype(F32)
            other = strips[0, t].astype(F32)
            finished[t, high] = ((1.0 - vshare) * own + vshare * other).astype(BF16)

        to_owner(i).start()

    update(0)
    to_side.start()
    for i in range(1, nslot):
        update(i)
        if i == 1:
            to_side.wait_recv()
        across(i - 1)
        if i > 1:
            downward(i - 2)
    across(nslot - 1)
    downward(nslot - 2)
    downward(nslot - 1)

    start = x * even
    if groups == 1:
        for s in range(nslot):
            got = finished[jnp.clip(start + s, 0, nslot - 1)]
            out_ref[s, :, half_m] = jnp.where(s < own_count, got, jnp.zeros_like(got))
    for i in range(nslot):
        to_owner(i).wait_recv()
    for s in range(nslot):
        got = partner_done[jnp.clip(start + s, 0, nslot - 1)]
        if groups == 1:
            out_ref[s, :, half_o] = jnp.where(s < own_count, got, jnp.zeros_like(got))
        else:
            own = finished[jnp.clip(start + s, 0, nslot - 1)]
            got = merge(own.astype(F32), got.astype(F32)).astype(BF16)
            out_ref[s] = jnp.where(s < own_count, got, jnp.zeros_like(got))

    to_side.wait_send()
    for c in out_swaps:
        c.wait_send()
    for c in sends:
        c.wait_send()
    for i in range(nslot):
        to_owner(i).wait_send()
        core_sum(i, 0).wait_send()
        core_sum(i, 1).wait_send()
        far_sum(i).wait_send()
        share_heads(i).wait_send()

    def drain(s, _):
        for kind, buf in ((0, wq), (1, wo)):
            for h in range(parts[kind]):
                line_do(buf, kind, s, h, lambda c: c.wait_send())
        return 0

    lax.fori_loop(0, planes - 1, drain, 0)


def on_device(regions, tile_data, tile_counts, modulation, qkv_weight, out_weight, blend_weights):
    nslot, tok, wide = tile_data.shape
    rows, kinds, _ = qkv_weight.shape
    fb = wide // 2
    width = modulation.shape[2]
    nblock = width // fb
    planes = regions // 2
    wqkv = qkv_weight.transpose(1, 0, 2)
    vmem = pl.BlockSpec(memory_space=pltpu.VMEM)
    smem = pl.BlockSpec(memory_space=pltpu.SMEM)
    dma = pltpu.SemaphoreType.DMA
    return pl.pallas_call(
        functools.partial(kernel, regions),
        out_shape=jax.ShapeDtypeStruct(tile_data.shape, BF16),
        in_specs=[smem, smem, vmem, vmem, vmem, vmem],
        out_specs=vmem,
        scratch_shapes=[
            pltpu.VMEM((2, nslot, tok, fb), BF16),
            pltpu.VMEM((nblock, nslot, tok, fb), BF16),
            pltpu.VMEM((2, 16, width), BF16),
            pltpu.VMEM((rows, kinds * fb), BF16),
            pltpu.VMEM((width, kinds * fb), BF16),
            pltpu.VMEM((planes * rows, wide), BF16),
            pltpu.VMEM((nslot, tok, width), BF16),
            pltpu.VMEM((nslot, tok, kinds * fb), F32),
            pltpu.VMEM((nslot, tok, wide), BF16),
            pltpu.VMEM((nslot, 2, tok, fb), BF16),
            pltpu.VMEM((nslot, tok, fb), BF16),
            pltpu.VMEM((nslot, 2, tok, fb), BF16),
            pltpu.VMEM((nslot, tok, fb), BF16),
            pltpu.VMEM((nslot, tok, fb), BF16),
            pltpu.VMEM((tok, fb), BF16),
            pltpu.VMEM((2, nslot, W * S, fb), BF16),
            pltpu.VMEM((nslot, tok, fb), BF16),
            pltpu.VMEM((nslot, tok, fb), BF16),
            dma((3,)),
            dma((3,)),
            dma((9,)),
            dma((9,)),
            dma((2, 2, planes - 1, 2)),
            dma((2, 2, planes - 1, 2)),
            dma((nslot,)),
            dma((nslot,)),
            dma((nslot, 2)),
            dma((nslot, 2)),
            dma((nslot,)),
            dma((nslot,)),
            dma((1,)),
            dma((1,)),
            dma((2, nslot)),
            dma((2, nslot)),
            dma((nslot,)),
            dma((nslot,)),
        ],
        compiler_params=pltpu.CompilerParams(
            collective_id=0, has_side_effects=True, vmem_limit_bytes=56 * 1024 * 1024
        ),
    )(tile_counts, blend_weights, tile_data, modulation, wqkv, out_weight)


def solution(mesh):
    return jax.shard_map(
        functools.partial(on_device, mesh.shape["region"]),
        mesh=mesh,
        in_specs=(
            P("region", None, "mp"),
            P(),
            P("region", None, None),
            P("region", None, "mp"),
            P("region", "mp"),
            P(),
        ),
        out_specs=P("region", None, "mp"),
        check_vma=False,
    )
```

```python
import functools
import math

import jax
import jax.numpy as jnp
from jax import lax
from jax.experimental import pallas as pl
from jax.experimental.pallas import tpu as pltpu
from jax.sharding import PartitionSpec as P

HDIM = 128
S = 16
W = 6
TCOLS = 8
MESH = pl.DeviceIdType.MESH
F32 = jnp.float32
BF16 = jnp.bfloat16


def kernel(
    regions,
    counts_ref,
    blend_ref,
    tiles_ref,
    mod_ref,
    wqkv_ref,
    wout_ref,
    out_ref,
    slots,
    feats,
    mods,
    stage,
    wq,
    wo,
    hidden,
    partial,
    attended,
    part_near,
    part_far,
    from_core,
    from_far,
    updated,
    side,
    strips,
    finished,
    partner_done,
    swap_send,
    swap_recv,
    gather_send,
    gather_recv,
    line_send,
    line_recv,
    heads_send,
    heads_recv,
    near_send,
    near_recv,
    sum_send,
    sum_recv,
    edge_send,
    edge_recv,
    strip_send,
    strip_recv,
    last_send,
    last_recv,
):
    planes = regions // 2
    region = lax.axis_index("region")
    mp = lax.axis_index("mp")
    plane = region // 2
    x = region % 2
    xo = 1 - x
    partner = plane * 2 + xo
    core = mp % 2
    yy = mp // 2
    mp_core = yy * 2 + (1 - core)
    mp_y = (1 - yy) * 2 + core
    nslot, tok, wide = tiles_ref.shape
    fb = wide // 2
    kinds, rows = wqkv_ref.shape[:2]
    down = TCOLS // nslot
    mine = mp * 2 + x
    has_up = plane > 0
    has_down = plane < planes - 1
    far_up = plane >= down
    far_down = plane < planes - down

    barrier = pltpu.get_barrier_semaphore()

    def greet(r, m):
        pl.semaphore_signal(barrier, inc=1, device_id=(r, m), device_id_type=MESH)

    greet(region, mp_core)
    greet(region, mp_y)
    greet(partner, mp)
    greet(partner, mp_y)
    for cond, step in ((has_up, -2), (has_down, 2), (far_up, -2 * down), (far_down, 2 * down)):

        @pl.when(cond)
        def _(step=step):
            greet(region + step, mp)

    arrivals = (
        4
        + has_up.astype(jnp.int32)
        + has_down.astype(jnp.int32)
        + far_up.astype(jnp.int32)
        + far_down.astype(jnp.int32)
    )
    half_o = pl.ds(pl.multiple_of(xo * fb, fb), fb)
    half_m = pl.ds(pl.multiple_of(x * fb, fb), fb)
    for k in range(kinds):
        at = slice(k * fb, (k + 1) * fb)
        wq[pl.ds(pl.multiple_of(region * rows, rows), rows), at] = wqkv_ref[k, :, half_m]
        stage[:, at] = wqkv_ref[k, :, half_o]
    wo[pl.ds(pl.multiple_of(plane * rows, rows), rows)] = wout_ref[...]
    pl.semaphore_wait(barrier, arrivals)

    def remote(src, dst, ssem, rsem, r, m):
        return pltpu.make_async_remote_copy(
            src_ref=src, dst_ref=dst, send_sem=ssem, recv_sem=rsem, device_id=(r, m), device_id_type=MESH
        )

    def block(buf, r):
        return buf.at[pl.ds(pl.multiple_of(r * rows, rows), rows)]

    def swap(i, src, dst):
        return remote(src, dst, swap_send.at[i], swap_recv.at[i], partner, mp)

    def swaps(r, g):
        return (
            swap(0, stage, block(wq, r)),
            swap(1, tiles_ref.at[:, :, half_o], slots.at[g]),
            swap(2, mods.at[g], mods.at[g]),
        )

    out_swaps = swaps(region, x)
    in_swaps = swaps(partner, xo)
    out_swaps[0].start()

    def line(buf, kind, way, s, h, q):
        ref = block(buf, 2 * q + h) if kind == 0 else block(buf, q)
        step = 2 if way == 0 else -2
        return remote(
            ref, ref, line_send.at[way, kind, s, h], line_recv.at[way, kind, s, h], region + step, mp
        )

    parts = (2, 1)

    def line_do(buf, kind, s, h, act):
        @pl.when(has_down & (plane - s >= 0))
        def _():
            act(line(buf, kind, 0, s, h, plane - s))

        @pl.when(has_up & (plane + s <= planes - 1))
        def _():
            act(line(buf, kind, 1, s, h, plane + s))

    def line_send_start(buf, kind, s, h):
        line_do(buf, kind, s, h, lambda c: c.start())

    def line_forward(buf, kind, s, h):
        @pl.when(plane - s - 1 >= 0)
        def _():
            line(buf, kind, 0, s, h, plane - s - 1).wait_recv()

        @pl.when(plane + s + 1 <= planes - 1)
        def _():
            line(buf, kind, 1, s, h, plane + s + 1).wait_recv()

        @pl.when(s + 1 < planes - 1)
        def _():
            line_send_start(buf, kind, s + 1, h)

    def forward_wq(s):
        line_forward(wq, 0, s, x)
        line_forward(wq, 0, s, xo)

    def forward_wo(s):
        line_forward(wo, 1, s, 0)

    line_send_start(wq, 0, 0, x)
    mods[x, 0:3, :] = mod_ref[0]
    slots[x] = tiles_ref[:, :, half_m]
    in_swaps[0].wait_recv()
    line_send_start(wq, 0, 0, xo)
    for c in out_swaps[1:]:
        c.start()
    line_forward(wq, 0, 0, x)

    in_swaps[1].wait_recv()
    even = counts_ref[2 * plane]
    own_count = counts_ref[region]
    for k in range(nslot):
        first = slots[0, k]
        second = slots[1, jnp.clip(k - even, 0, nslot - 1)]
        feats[mine, k] = jnp.where(k < even, first, second)

    def gather(i, b, r, m):
        return remote(feats.at[b], feats.at[b], gather_send.at[i], gather_recv.at[i], r, m)

    from_x, from_y, diagonal = mp * 2 + xo, mp_y * 2 + x, mp_y * 2 + xo
    core_blocks = (mp_core * 2 + x, mp_core * 2 + xo, (3 - mp) * 2 + x, (3 - mp) * 2 + xo)
    half = nslot // 2

    def gather_half(i, b, r, m):
        ref = feats.at[b, pl.ds(i * half, half)]
        return remote(ref, ref, gather_send.at[7 + i], gather_recv.at[7 + i], r, m)

    sends = [
        gather(0, mine, partner, mp),
        gather(1, mine, region, mp_y),
        gather(3, mine, region, mp_core),
    ]
    for c in sends:
        c.start()
    line_forward(wq, 0, 0, xo)
    line_forward(wq, 0, 1, x)
    gather(0, from_x, partner, mp).wait_recv()
    gather(1, from_y, region, mp_y).wait_recv()
    passed = [
        gather_half(0, from_y, partner, mp),
        gather_half(1, from_x, region, mp_y),
        gather(4, from_x, region, mp_core),
        gather(5, from_y, region, mp_core),
    ]
    for c in passed:
        c.start()
    sends += passed
    line_forward(wq, 0, 1, xo)
    line_send_start(wo, 1, 0, 0)
    gather_half(0, diagonal, partner, mp).wait_recv()
    gather_half(1, diagonal, region, mp_y).wait_recv()
    c = gather(6, diagonal, region, mp_core)
    c.start()
    sends.append(c)
    in_swaps[2].wait_recv()
    for i in range(4):
        gather(3 + i, core_blocks[i], region, mp_core).wait_recv()

    nblock = feats.shape[0]
    inv = 1.0 / (nblock * fb)
    shift_e, gain_e = mods[0].astype(F32)[0:1], 1.0 + mods[0].astype(F32)[1:2]
    shift_d, gain_d = mods[1].astype(F32)[0:1], 1.0 + mods[1].astype(F32)[1:2]
    lines = 64
    chunks = tok // lines

    def normalise(i, _):
        t = i // chunks
        at_rows = pl.ds(pl.multiple_of((i % chunks) * lines, lines), lines)
        total = feats[0, t, at_rows].astype(F32)
        for b in range(1, nblock):
            total = total + feats[b, t, at_rows].astype(F32)
        mean = jnp.sum(total, axis=1, keepdims=True) * inv
        total = jnp.zeros((lines, fb), F32)
        for b in range(nblock):
            c = feats[b, t, at_rows].astype(F32) - mean
            total = total + c * c
        scale = lax.rsqrt(jnp.sum(total, axis=1, keepdims=True) * inv + 1e-06)
        shift = jnp.where(t < even, shift_e, shift_d)
        gain = jnp.where(t < even, gain_e, gain_d)
        for b in range(nblock):
            at = slice(b * fb, (b + 1) * fb)
            c = (feats[b, t, at_rows].astype(F32) - mean) * scale
            hidden[t, at_rows, at] = (c * gain[:, at] + shift[:, at]).astype(BF16)
        return 0

    lax.fori_loop(0, nslot * chunks, normalise, 0)

    latest = jnp.where(plane < planes // 2, 3, 0)
    group = feats.shape[0] * fb // 4

    def multiply(t, g):
        at = pl.ds(pl.multiple_of(g * group, group), group)
        return jnp.dot(hidden[t, :, at], wq[at], preferred_element_type=F32)

    def begin(t, _):
        total = multiply(t, (latest + 1) % 4) + multiply(t, (latest + 2) % 4)
        partial[t] = total + multiply(t, (latest + 3) % 4)
        return 0

    def more(s, _):
        forward_wq(s)
        forward_wo(s - 2)
        return 0

    lax.fori_loop(2, planes - 2, more, 0)
    lax.fori_loop(0, nslot, begin, 0)
    forward_wq(planes - 2)

    heads = fb // HDIM

    def attend(t, _):
        outs = []
        proj = (partial[t] + multiply(t, latest)).astype(BF16)
        for h in range(heads):
            q = proj[:, h * HDIM : (h + 1) * HDIM]
            k = proj[:, fb + h * HDIM : fb + (h + 1) * HDIM]
            v = proj[:, 2 * fb + h * HDIM : 2 * fb + (h + 1) * HDIM]
            scores = lax.dot_general(q, k, (((1,), (1,)), ((), ())), preferred_element_type=F32)
            e = jnp.exp((scores - jnp.max(scores, axis=-1, keepdims=True)) * (1.0 / math.sqrt(HDIM)))
            p = (e * (1.0 / jnp.sum(e, axis=-1, keepdims=True))).astype(BF16)
            outs.append(jnp.dot(p, v, preferred_element_type=F32).astype(BF16))
        attended[t, :, half_m] = jnp.concatenate(outs, axis=1)
        return 0

    odd = plane % 2

    def tile_at(i):
        return i * odd + (nslot - 1 - i) * (1 - odd)

    def share_heads(i):
        ref = attended.at[tile_at(i), :, half_m]
        return remote(ref, ref, heads_send.at[i], heads_recv.at[i], partner, mp)

    def other_heads(i):
        ref = attended.at[tile_at(i), :, half_o]
        return remote(ref, ref, heads_send.at[i], heads_recv.at[i], partner, mp)

    def attend_at(i, _):
        attend(tile_at(i), 0)
        share_heads(i).start()
        return 0

    attend_at(0, 0)
    forward_wo(planes - 4)
    lax.fori_loop(1, nslot - 1, attend_at, 0)
    forward_wo(planes - 3)
    attend_at(nslot - 1, 0)

    def product(m, t):
        w = wo[pl.ds(pl.multiple_of(m * fb, fb), fb)]
        return lax.dot_general(attended[t], w, (((1,), (1,)), ((), ())), preferred_element_type=F32)

    def core_sum(i, j):
        t = tile_at(i)
        return remote(
            part_near.at[t, j],
            from_core.at[t, j],
            near_send.at[i, j],
            near_recv.at[i, j],
            region,
            mp_core,
        )

    def far_sum(i):
        t = tile_at(i)
        return remote(part_far.at[t], from_far.at[t], sum_send.at[i], sum_recv.at[i], region, mp_y)

    def near(i, wanted):
        t = tile_at(i)
        for j, m in ((0, 3 - mp), (1, mp_core)):

            @pl.when(wanted(m))
            def _(j=j, m=m):
                part_near[t, j] = product(m, t).astype(BF16)
                core_sum(i, j).start()

    def far(i, wanted):
        t = tile_at(i)

        @pl.when(wanted(mp_y))
        def _():
            core_sum(i, 0).wait_recv()
            part_far[t] = (product(mp_y, t) + from_core[t, 0].astype(F32)).astype(BF16)
            far_sum(i).start()

    def early(m):
        return m != latest

    def late(m):
        return m == latest

    for i in range(nslot):
        other_heads(i).wait_recv()
        near(i, early)
        if i > 0:
            far(i - 1, early)
    far(nslot - 1, early)
    forward_wo(planes - 2)
    for i in range(nslot):
        near(i, late)
        far(i, late)

    groups = fb // rows

    def pick(lo, hi):
        if groups == 1:
            return jnp.where(x == 0, lo, hi)
        both = jnp.concatenate([lo, hi], axis=1)
        cols = [both[:, g * rows : (g + 1) * rows] for g in range(2 * groups)]
        return jnp.concatenate(
            [jnp.where(x == 0, cols[2 * g], cols[2 * g + 1]) for g in range(groups)], axis=1
        )

    def merge(own, other):
        evens = jnp.where(x == 0, own, other)
        odds = jnp.where(x == 0, other, own)
        if groups == 1:
            return jnp.concatenate([evens, odds], axis=1)
        cols = []
        for g in range(groups):
            at = slice(g * rows, (g + 1) * rows)
            cols += [evens[:, at], odds[:, at]]
        return jnp.concatenate(cols, axis=1)

    def gate_of(g):
        lo = pl.ds(pl.multiple_of(mp * 2 * fb, fb), fb)
        hi = pl.ds(pl.multiple_of(mp * 2 * fb + fb, fb), fb)
        return pick(mods[g, :, lo].astype(F32), mods[g, :, hi].astype(F32))[2:3]

    gate_e = gate_of(0)
    gate_d = gate_of(1)

    def update(i):
        t = tile_at(i)
        total = product(mp, t)
        core_sum(i, 1).wait_recv()
        total = total + from_core[t, 1].astype(F32)
        far_sum(i).wait_recv()
        total = total + from_far[t].astype(F32)
        gate = jnp.where(t < even, gate_e, gate_d)
        if groups == 1:
            tile = feats[mine, t].astype(F32)
        else:
            tile = pick(feats[2 * mp, t].astype(F32), feats[2 * mp + 1, t].astype(F32))
        updated[t] = (tile + gate * total).astype(BF16)

    to_side = remote(
        updated.at[tile_at(0)],
        side,
        edge_send.at[0],
        edge_recv.at[0],
        region + 2 - 4 * odd,
        mp,
    )
    col = lax.broadcasted_iota(jnp.int32, (tok, fb), 0) % S
    share = jnp.zeros((tok, fb), F32)
    for k in range(W):
        share = jnp.where((col == k) | (col == S - W + k), blend_ref[k], share)
    near_cols = col < W
    far_cols = col >= S - W

    def across(i):
        t = tile_at(i)
        own = updated[t].astype(F32)
        if i > 0:
            before = updated[tile_at(i - 1)].astype(F32)
        else:
            before = side[...].astype(F32)
        if i < nslot - 1:
            after = updated[tile_at(i + 1)].astype(F32)
            has_left = has_right = True
        else:
            after = own
            has_left, has_right = odd == 1, odd == 0
        left = jnp.where(odd == 1, before, after)
        right = jnp.where(odd == 1, after, before)
        left = pltpu.roll(left, tok - (S - W), 0)
        right = pltpu.roll(right, S - W, 0)
        new = jnp.where(near_cols & has_left, (1.0 - share) * left + share * own, own)
        new = jnp.where(far_cols & has_right, (1.0 - share) * own + share * right, new)
        finished[t] = new.astype(BF16)

        @pl.when(far_up)
        def _():
            to_above(i).start()

        @pl.when(far_down)
        def _():
            to_below(i).start()

    reach = W * S
    low = pl.ds(0, reach)
    high = pl.ds(tok - reach, reach)

    def to_above(i):
        t = tile_at(i)
        return remote(
            finished.at[t, low],
            strips.at[0, t],
            strip_send.at[0, i],
            strip_recv.at[0, i],
            region - 2 * down,
            mp,
        )

    def to_below(i):
        t = tile_at(i)
        return remote(
            finished.at[t, high],
            strips.at[1, t],
            strip_send.at[1, i],
            strip_recv.at[1, i],
            region + 2 * down,
            mp,
        )

    row = lax.broadcasted_iota(jnp.int32, (reach, fb), 0) // S
    vshare = jnp.zeros((reach, fb), F32)
    for k in range(W):
        vshare = jnp.where(row == k, blend_ref[k], vshare)

    def to_owner(i):
        t = tile_at(i)
        return remote(
            finished.at[t], partner_done.at[t], last_send.at[i], last_recv.at[i], partner, mp
        )

    def downward(i):
        t = tile_at(i)

        @pl.when(far_up)
        def _():
            to_above(i).wait_send()
            to_below(i).wait_recv()
            own = finished[t, low].astype(F32)
            other = strips[1, t].astype(F32)
            finished[t, low] = ((1.0 - vshare) * other + vshare * own).astype(BF16)

        @pl.when(far_down)
        def _():
            to_below(i).wait_send()
            to_above(i).wait_recv()
            own = finished[t, high].astype(F32)
            other = strips[0, t].astype(F32)
            finished[t, high] = ((1.0 - vshare) * own + vshare * other).astype(BF16)

        to_owner(i).start()

    update(0)
    to_side.start()
    for i in range(1, nslot):
        update(i)
        if i == 1:
            to_side.wait_recv()
        across(i - 1)
        if i > 1:
            downward(i - 2)
    across(nslot - 1)
    downward(nslot - 2)
    downward(nslot - 1)

    start = x * even
    if groups == 1:
        for s in range(nslot):
            got = finished[jnp.clip(start + s, 0, nslot - 1)]
            out_ref[s, :, half_m] = jnp.where(s < own_count, got, jnp.zeros_like(got))
    for i in range(nslot):
        to_owner(i).wait_recv()
    for s in range(nslot):
        got = partner_done[jnp.clip(start + s, 0, nslot - 1)]
        if groups == 1:
            out_ref[s, :, half_o] = jnp.where(s < own_count, got, jnp.zeros_like(got))
        else:
            own = finished[jnp.clip(start + s, 0, nslot - 1)]
            got = merge(own.astype(F32), got.astype(F32)).astype(BF16)
            out_ref[s] = jnp.where(s < own_count, got, jnp.zeros_like(got))

    to_side.wait_send()
    for c in out_swaps:
        c.wait_send()
    for c in sends:
        c.wait_send()
    for i in range(nslot):
        to_owner(i).wait_send()
        core_sum(i, 0).wait_send()
        core_sum(i, 1).wait_send()
        far_sum(i).wait_send()
        share_heads(i).wait_send()

    def drain(s, _):
        for kind, buf in ((0, wq), (1, wo)):
            for h in range(parts[kind]):
                line_do(buf, kind, s, h, lambda c: c.wait_send())
        return 0

    lax.fori_loop(0, planes - 1, drain, 0)


def on_device(regions, tile_data, tile_counts, modulation, qkv_weight, out_weight, blend_weights):
    nslot, tok, wide = tile_data.shape
    rows, kinds, _ = qkv_weight.shape
    fb = wide // 2
    width = modulation.shape[2]
    nblock = width // fb
    planes = regions // 2
    wqkv = qkv_weight.transpose(1, 0, 2)
    vmem = pl.BlockSpec(memory_space=pltpu.VMEM)
    smem = pl.BlockSpec(memory_space=pltpu.SMEM)
    dma = pltpu.SemaphoreType.DMA
    return pl.pallas_call(
        functools.partial(kernel, regions),
        out_shape=jax.ShapeDtypeStruct(tile_data.shape, BF16),
        in_specs=[smem, smem, vmem, vmem, vmem, vmem],
        out_specs=vmem,
        scratch_shapes=[
            pltpu.VMEM((2, nslot, tok, fb), BF16),
            pltpu.VMEM((nblock, nslot, tok, fb), BF16),
            pltpu.VMEM((2, 16, width), BF16),
            pltpu.VMEM((rows, kinds * fb), BF16),
            pltpu.VMEM((width, kinds * fb), BF16),
            pltpu.VMEM((planes * rows, wide), BF16),
            pltpu.VMEM((nslot, tok, width), BF16),
            pltpu.VMEM((nslot, tok, kinds * fb), F32),
            pltpu.VMEM((nslot, tok, wide), BF16),
            pltpu.VMEM((nslot, 2, tok, fb), BF16),
            pltpu.VMEM((nslot, tok, fb), BF16),
            pltpu.VMEM((nslot, 2, tok, fb), BF16),
            pltpu.VMEM((nslot, tok, fb), BF16),
            pltpu.VMEM((nslot, tok, fb), BF16),
            pltpu.VMEM((tok, fb), BF16),
            pltpu.VMEM((2, nslot, W * S, fb), BF16),
            pltpu.VMEM((nslot, tok, fb), BF16),
            pltpu.VMEM((nslot, tok, fb), BF16),
            dma((3,)),
            dma((3,)),
            dma((9,)),
            dma((9,)),
            dma((2, 2, planes - 1, 2)),
            dma((2, 2, planes - 1, 2)),
            dma((nslot,)),
            dma((nslot,)),
            dma((nslot, 2)),
            dma((nslot, 2)),
            dma((nslot,)),
            dma((nslot,)),
            dma((1,)),
            dma((1,)),
            dma((2, nslot)),
            dma((2, nslot)),
            dma((nslot,)),
            dma((nslot,)),
        ],
        compiler_params=pltpu.CompilerParams(
            collective_id=0, has_side_effects=True, vmem_limit_bytes=56 * 1024 * 1024
        ),
    )(tile_counts, blend_weights, tile_data, modulation, wqkv, out_weight)


def solution(mesh):
    return jax.shard_map(
        functools.partial(on_device, mesh.shape["region"]),
        mesh=mesh,
        in_specs=(
            P("region", None, "mp"),
            P(),
            P("region", None, None),
            P("region", None, "mp"),
            P("region", "mp"),
            P(),
        ),
        out_specs=P("region", None, "mp"),
        check_vma=False,
    )
```
